32 devices in a mesh: grp: 2 (over x), ma: 16 (over z, y, core).
Axes of the slice: x: 2, y: 2, z: 4, core: 2. Of those that a mesh axis runs over, the one named last changes fastest.
Arguments:
- vis: float32 [16384, 2, 256], P(('grp', 'ma')), parts along dimension 0, may hold values from -6 to 6
- transfer: bfloat16 [32, 2, 256, 1024], P(('grp', 'ma')), parts along dimension 0, may hold values from -0.1875 to 0.1875
- band_start: int32 [2], P('grp'), parts along dimension 0, may hold values from 0 to 8176
- comp_index: int32 [2048], P(('grp', 'ma')), parts along dimension 0, may hold values from 0 to 16383
- comp_amp: int32 [2048, 2], P(('grp', 'ma')), parts along dimension 0, may hold values from -4096 to 4096
Outputs:
- residual_alm: float32 [32, 2, 1024], P(('grp', 'ma')), parts along dimension 0
The draws below stay inside these ranges and needn't reach their ends.
There are 2 independent parts, one for each index of `grp`. The reference program is written for one: setup_inputs(seed, part) draws one part's arguments, and reference() takes and returns one part's arrays. A program takes and returns all parts, laid end to end along the dimension named above; each array names one. Nothing has to cross between parts.
All inputs are finite; a program needn't handle non-finite values.
Results may differ from the reference program's by a relative error of at most 0.003.
Values sent between devices are 32-bit elements; how exact they have to be, the bound alone decides.
A program may use at most 64 MiB of HBM per device.

```python
import math
import jax
import jax.numpy as jnp
from jax import lax

SIDEREAL_TICKS = 8192
L = 1024
BL = 256
MBAND = 16
NCOMP = 1024


def plant(result, stream_key, low, top_value):
    spot = [jax.random.randint(jax.random.fold_in(stream_key, axis), (), 0, length) for axis, length in enumerate(result.shape)]
    longest = result.shape.index(max(result.shape))
    beside = spot[:longest] + [(spot[longest] + 1) % result.shape[longest]] + spot[longest + 1:]
    return result.at[tuple(spot)].set(low).at[tuple(beside)].set(top_value)


def shard_levels(own_key, extent, shards, low, high):
    gain, own = 1.0, jax.random.fold_in(own_key, 6)
    for position, blocks in shards:
        draws = jnp.exp(jax.random.uniform(jax.random.fold_in(own, position), (blocks,), jnp.float32, low / len(shards), high / len(shards)))
        gain = gain * jnp.repeat(draws, extent[position] // blocks).reshape([-1 if axis == position else 1 for axis in range(len(extent))])
    return gain


def centred(stream_key, extent, scale, limit, pieces=(), kind=jnp.bfloat16):
    array = scale * jax.random.normal(stream_key, extent, jnp.float32)
    if pieces:
        array = array * shard_levels(stream_key, extent, pieces, -0.22, 0.18)
    return jnp.clip(array, -limit, limit).astype(kind)


def setup_inputs(seed: int = 0, part: int = 0) -> dict:
    key_list = jax.random.split(jax.random.key(seed), 6)
    part_keys = jax.random.split(jax.random.fold_in(key_list[5], part), 6)
    return {
        "vis": centred(part_keys[0], (SIDEREAL_TICKS, 2, BL), 1.0, 6.0, ((0, 16),), jnp.float32),
        "transfer": centred(part_keys[1], (MBAND, 2, BL, L), L ** -0.5, 0.1875, ((0, 16),)),
        "band_start": jax.random.randint(part_keys[2], (1,), 0, SIDEREAL_TICKS - MBAND + 1).astype(jnp.int32),
        "comp_index": plant(jax.random.randint(part_keys[3], (NCOMP,), 0, MBAND * L), jax.random.fold_in(part_keys[3], 1), 0, (MBAND * L) - 1).astype(jnp.int32),
        "comp_amp": plant(jax.random.randint(part_keys[4], (NCOMP, 2), -4096, 4097), jax.random.fold_in(part_keys[4], 1), -4096, 4096).astype(jnp.int32),
    }


def transform(vis, band_start):
    tick_moments = jnp.arange(SIDEREAL_TICKS, dtype=jnp.int32)
    azimuthal_orders = band_start[0] + jnp.arange(MBAND, dtype=jnp.int32)
    rotation_radians = azimuthal_orders[:, None] * tick_moments[None, :] % SIDEREAL_TICKS
    angle = rotation_radians.astype(jnp.float32) * (2.0 * math.pi / SIDEREAL_TICKS)
    trig_pair = jnp.concatenate([jnp.cos(angle), jnp.sin(angle)], 0)
    flat_visibility = vis.reshape(SIDEREAL_TICKS, 2 * BL)
    product = jnp.dot(trig_pair, flat_visibility, precision=lax.Precision.HIGHEST, preferred_element_type=jnp.float32)
    product = product.reshape(2, MBAND, 2, BL)
    scale = 1.0 / math.sqrt(SIDEREAL_TICKS)
    real_part = (product[0, :, 0] + product[1, :, 1]) * scale
    imag_part = (product[0, :, 1] - product[1, :, 0]) * scale
    return jnp.stack([real_part, imag_part], 1)

def one_mode(item):
    matrix, alm, spectrum = item
    wide = matrix.astype(jnp.float32)
    flat_matrix = wide.reshape(2 * BL, L)
    predicted = jnp.dot(flat_matrix, alm.astype(jnp.float32), precision=lax.Precision.HIGHEST).reshape(2, BL, 2)
    pred_real = predicted[0, :, 0] - predicted[1, :, 1]
    pred_imag = predicted[0, :, 1] + predicted[1, :, 0]
    resid_vis = (spectrum - jnp.stack([pred_real, pred_imag], 0)).astype(jnp.bfloat16)
    resid_vis = lax.optimization_barrier(resid_vis).astype(jnp.float32)
    columns = jnp.transpose(wide, (1, 0, 2)).reshape(BL, 2 * L)
    projected = jnp.dot(resid_vis, columns, precision=lax.Precision.HIGHEST).reshape(2, 2, L)
    alm_real = projected[0, 0] + projected[1, 1]
    alm_imag = projected[1, 0] - projected[0, 1]
    return jnp.stack([alm_real, alm_imag], 0)

def reference(vis, transfer, band_start, comp_index, comp_amp):
    spectra = transform(vis, band_start)
    summed = jax.ops.segment_sum(comp_amp, comp_index, num_segments=MBAND * L)
    model_alm = (summed.astype(jnp.float32) * (1.0 / 1024.0)).astype(jnp.bfloat16)
    model_alm = lax.optimization_barrier(model_alm).reshape(MBAND, L, 2)
    return lax.map(one_mode, (transfer, model_alm, spectra))
```

```python
import functools
import math

import jax
import jax.numpy as jnp
from jax import lax
from jax.experimental import pallas as pl
from jax.experimental.pallas import tpu as pltpu
from jax.sharding import PartitionSpec as P

LANES = 128
F32 = jnp.float32
BF16 = jnp.bfloat16
MESH = pl.DeviceIdType.MESH


def trig_pair(order_start, tick_start, modes, ticks, period):
    order = order_start + lax.broadcasted_iota(jnp.int32, (modes, ticks), 0)
    tick = tick_start + lax.broadcasted_iota(jnp.int32, (modes, ticks), 1)
    phase = (order * tick) & (period - 1)
    quarter = period // 4
    shift = quarter.bit_length() - 1
    quadrant = (phase + quarter // 2) >> shift
    x = (phase - (quadrant << shift)).astype(F32) * (2.0 * math.pi / period)
    z = x * x
    sin_x = x * (1.0 + z * (-1.0 / 6 + z * (1.0 / 120 + z * (-1.0 / 5040 + z * (1.0 / 362880)))))
    cos_x = 1.0 + z * (-0.5 + z * (1.0 / 24 + z * (-1.0 / 720 + z * (1.0 / 40320))))
    swap = (quadrant & 1) == 1
    cos = jnp.where(swap, sin_x, cos_x)
    sin = jnp.where(swap, cos_x, sin_x)
    cos = jnp.where(((quadrant + 1) & 2) == 2, -cos, cos)
    sin = jnp.where((quadrant & 2) == 2, -sin, sin)
    return cos, sin


def split(values):
    high = values.astype(BF16)
    return high, (values - high.astype(F32)).astype(BF16)


def mul(a, b, contract=((1,), (0,))):
    return lax.dot_general(a, b, (contract, ((), ())), preferred_element_type=F32)


def kernel(
    n, ticks, tiles, count, width,
    vis_hbm, transfer_hbm, start_ref, index_ref, amp_ref, out_ref,
    vis, transfer, comp_out, comp_in, spec_out, spec_in,
    vis_sem, transfer_sem, comp_send, comp_recv, spec_send, spec_recv,
):
    me = lax.axis_index("ma")
    vis_copy = pltpu.make_async_copy(vis_hbm, vis, vis_sem)
    transfer_copy = pltpu.make_async_copy(transfer_hbm, transfer, transfer_sem)
    vis_copy.start()
    transfer_copy.start()

    def peers(step):
        if n <= 32:
            for offset in range(1, n):
                step(offset)
        else:
            pl.loop(1, n)(step)

    def peer(offset):
        target = me + offset
        return jnp.where(target >= n, target - n, target)

    barrier = pltpu.get_barrier_semaphore()

    def greet(offset):
        pl.semaphore_signal(barrier, inc=1, device_id={"ma": peer(offset)}, device_id_type=MESH)

    peers(greet)

    comp_out[...] = jnp.full(comp_out.shape, -1, jnp.int32)
    comp_out[0:1, 0:count] = index_ref[...]
    comp_out[1:3, 0:count] = amp_ref[...]
    comp_in[n - 1] = comp_out[...]
    pl.semaphore_wait(barrier, n - 1)

    def send_comp(offset):
        pltpu.make_async_remote_copy(
            src_ref=comp_out, dst_ref=comp_in.at[offset - 1],
            send_sem=comp_send, recv_sem=comp_recv,
            device_id={"ma": peer(offset)}, device_id_type=MESH,
        ).start()

    peers(send_comp)

    cos, sin = trig_pair(start_ref[0], me * ticks, n, ticks, ticks * n)
    (cos_high, cos_low), (sin_high, sin_low) = split(cos), split(sin)
    high_rows = jnp.concatenate([cos_high, sin_high], 0)
    all_rows = jnp.concatenate([cos_high, sin_high, cos_low, sin_low], 0)
    vis_copy.wait()
    rows = 2 * tiles
    for tile in range(tiles):
        parts = [vis[pl.ds(2 * tile + c, ticks, stride=rows), :] for c in range(2)]
        high, low = split(jnp.concatenate(parts, 1))
        product = mul(all_rows, high)
        product = product[: 2 * n] + product[2 * n :] + mul(high_rows, low)
        real = product[:n, :LANES] + product[n:, LANES:]
        imag = product[:n, LANES:] - product[n:, :LANES]
        spec_out[:, tile, :] = real
        spec_out[:, tiles + tile, :] = imag

    def send_spec(offset):
        pltpu.make_async_remote_copy(
            src_ref=spec_out.at[peer(offset)], dst_ref=spec_in.at[offset - 1],
            send_sem=spec_send, recv_sem=spec_recv,
            device_id={"ma": peer(offset)}, device_id_type=MESH,
        ).start()

    peers(send_spec)

    arrived = comp_in.at[pl.ds(0, n - 1)]
    pltpu.make_async_copy(arrived, arrived, comp_recv).wait()
    fields = [comp_in[:, row, :] for row in range(3)]
    if 2 * count == LANES and n % 2 == 0:
        fields = [jnp.concatenate([f[: n // 2, :count], f[n // 2 :, :count]], 1) for f in fields]
    index = fields[0] - me * width
    blocks = width // LANES
    row_id = lax.broadcasted_iota(jnp.int32, (2 * blocks, LANES), 0)
    low_id = lax.broadcasted_iota(jnp.int32, (LANES, LANES), 0)
    weights, places = [], []
    for chunk in range(index.shape[0]):
        at = index[chunk : chunk + 1]
        amp = jnp.where(
            (row_id & 1) == 1, fields[2][chunk : chunk + 1], fields[1][chunk : chunk + 1]
        )
        amp = jnp.where((at >> 7) == (row_id >> 1), amp, 0)
        halves = jnp.concatenate([amp >> 6, amp & 63], 0)
        weights.append(halves.astype(F32).astype(BF16))
        places.append(jnp.where((at & 127) == low_id, 1.0, 0.0).astype(BF16))
    halves = mul(jnp.concatenate(weights, 1), jnp.concatenate(places, 1), ((1,), (1,)))
    halves = halves.astype(jnp.int32)
    summed = halves[: 2 * blocks] * 64 + halves[2 * blocks :]
    model = summed.astype(F32) * (1.0 / 1024.0)
    model = jnp.concatenate([model[2 * i : 2 * i + 2] for i in range(blocks)], 1).astype(BF16)

    transfer_copy.wait()
    lines = tiles * LANES
    predicted = mul(model, transfer[...], ((1,), (1,)))
    pred_real = predicted[0:1, :lines] - predicted[1:2, lines:]
    pred_imag = predicted[1:2, :lines] + predicted[0:1, lines:]

    spec_in[n - 1] = spec_out[me]
    arrived = spec_in.at[pl.ds(0, n - 1)]
    pltpu.make_async_copy(arrived, arrived, spec_recv).wait()
    spectra = jnp.sum(spec_in[...], 0) * (1.0 / math.sqrt(ticks * n))
    real = jnp.concatenate([spectra[i : i + 1] for i in range(tiles)], 1)
    imag = jnp.concatenate([spectra[tiles + i : tiles + i + 1] for i in range(tiles)], 1)
    real, imag = real - pred_real, imag - pred_imag
    resid = jnp.concatenate(
        [jnp.concatenate([real, imag], 1), jnp.concatenate([imag, -real], 1)], 0
    ).astype(BF16)
    alm = mul(resid, transfer[...])
    for block in range(blocks):
        out_ref[2 * block : 2 * block + 2, :] = alm[:, block * LANES : (block + 1) * LANES]

    for buffer, sem in ((comp_in, comp_send), (spec_in, spec_send)):
        sent = buffer.at[pl.ds(0, n - 1)]
        pltpu.make_async_copy(sent, sent, sem).wait()


def body(vis, transfer, band_start, comp_index, comp_amp):
    n = lax.axis_size("ma")
    ticks, _, lines = vis.shape
    m_local, _, _, width = transfer.shape
    count = comp_index.shape[0]
    tiles = lines // LANES
    blocks = width // LANES
    assert m_local == 1 and lines % LANES == 0 and width % LANES == 0 and count <= LANES
    assert (ticks * n) & (ticks * n - 1) == 0
    flat_vis = (
        vis.reshape(ticks, 2, tiles, LANES).transpose(0, 2, 1, 3).reshape(ticks * 2 * tiles, LANES)
    )
    out = pl.pallas_call(
        functools.partial(kernel, n, ticks, tiles, count, width),
        out_shape=jax.ShapeDtypeStruct((2 * blocks, LANES), F32),
        in_specs=[
            pl.BlockSpec(memory_space=pl.ANY),
            pl.BlockSpec(memory_space=pl.ANY),
            pl.BlockSpec(memory_space=pltpu.SMEM),
            pl.BlockSpec(memory_space=pltpu.VMEM),
            pl.BlockSpec(memory_space=pltpu.VMEM),
        ],
        out_specs=pl.BlockSpec(memory_space=pltpu.VMEM),
        scratch_shapes=[
            pltpu.VMEM(flat_vis.shape, F32),
            pltpu.VMEM((2 * lines, width), BF16),
            pltpu.VMEM((4, LANES), jnp.int32),
            pltpu.VMEM((n, 4, LANES), jnp.int32),
            pltpu.VMEM((n, 2 * tiles, LANES), F32),
            pltpu.VMEM((n, 2 * tiles, LANES), F32),
        ]
        + [pltpu.SemaphoreType.DMA] * 6,
        compiler_params=pltpu.CompilerParams(
            collective_id=0, has_side_effects=True, vmem_limit_bytes=48 * 1024 * 1024
        ),
        cost_estimate=pl.CostEstimate(
            flops=2 * 2 * n * ticks * 2 * lines + 8 * lines * width * 2,
            bytes_accessed=vis.size * 4 + transfer.size * 2,
            transcendentals=0,
        ),
    )(
        flat_vis,
        transfer.reshape(2 * lines, width),
        band_start,
        comp_index.reshape(1, count),
        comp_amp.T,
    )
    return out.reshape(blocks, 2, LANES).transpose(1, 0, 2).reshape(1, 2, width)


def solution(mesh):
    in_specs = (
        P(("grp", "ma"), None, None),
        P(("grp", "ma"), None, None, None),
        P("grp"),
        P(("grp", "ma")),
        P(("grp", "ma"), None),
    )
    out_specs = P(("grp", "ma"), None, None)
    return jax.shard_map(body, mesh=mesh, in_specs=in_specs, out_specs=out_specs, check_vma=False)
```

```python
import functools
import math

import jax
import jax.numpy as jnp
from jax import lax
from jax.experimental import pallas as pl
from jax.experimental.pallas import tpu as pltpu
from jax.sharding import PartitionSpec as P

LANES = 128
F32 = jnp.float32
BF16 = jnp.bfloat16
MESH = pl.DeviceIdType.MESH


def trig_pair(order_start, tick_start, modes, ticks, period):
    order = order_start + lax.broadcasted_iota(jnp.int32, (modes, ticks), 0)
    tick = tick_start + lax.broadcasted_iota(jnp.int32, (modes, ticks), 1)
    phase = (order * tick) & (period - 1)
    quarter = period // 4
    shift = quarter.bit_length() - 1
    quadrant = (phase + quarter // 2) >> shift
    x = (phase - (quadrant << shift)).astype(F32) * (2.0 * math.pi / period)
    z = x * x
    sin_x = x * (1.0 + z * (-1.0 / 6 + z * (1.0 / 120 + z * (-1.0 / 5040 + z * (1.0 / 362880)))))
    cos_x = 1.0 + z * (-0.5 + z * (1.0 / 24 + z * (-1.0 / 720 + z * (1.0 / 40320))))
    swap = (quadrant & 1) == 1
    cos = jnp.where(swap, sin_x, cos_x)
    sin = jnp.where(swap, cos_x, sin_x)
    cos = jnp.where(((quadrant + 1) & 2) == 2, -cos, cos)
    sin = jnp.where((quadrant & 2) == 2, -sin, sin)
    return cos, sin


def split(values):
    high = values.astype(BF16)
    return high, (values - high.astype(F32)).astype(BF16)


def mul(a, b, contract=((1,), (0,))):
    return lax.dot_general(a, b, (contract, ((), ())), preferred_element_type=F32)


def kernel(
    n, ticks, tiles, count, width,
    vis_hbm, transfer_hbm, start_hbm, index_hbm, amp_hbm, out_ref,
    vis, transfer, start_ref, index_ref, amp_ref, comp_out, comp_in, spec_out, spec_in,
    vis_sem, transfer_sem, start_sem, index_sem, amp_sem,
    comp_send, comp_recv, spec_send, spec_recv,
):
    me = lax.axis_index("ma")
    start_copy = pltpu.make_async_copy(start_hbm, start_ref, start_sem)
    index_copy = pltpu.make_async_copy(index_hbm, index_ref, index_sem)
    amp_copy = pltpu.make_async_copy(amp_hbm, amp_ref, amp_sem)
    vis_copy = pltpu.make_async_copy(vis_hbm, vis, vis_sem)
    transfer_copy = pltpu.make_async_copy(transfer_hbm, transfer, transfer_sem)
    for copy in (start_copy, index_copy, amp_copy, vis_copy, transfer_copy):
        copy.start()

    def peers(step):
        if n <= 32:
            for offset in range(1, n):
                step(offset)
        else:
            pl.loop(1, n)(step)

    def peer(offset):
        target = me + offset
        return jnp.where(target >= n, target - n, target)

    barrier = pltpu.get_barrier_semaphore()

    def greet(offset):
        pl.semaphore_signal(barrier, inc=1, device_id={"ma": peer(offset)}, device_id_type=MESH)

    peers(greet)

    comp_out[...] = jnp.full(comp_out.shape, -1, jnp.int32)
    index_copy.wait()
    amp_copy.wait()
    comp_out[0:1, 0:count] = index_ref[...]
    comp_out[1:3, 0:count] = amp_ref[...]
    comp_in[n - 1] = comp_out[...]
    start_copy.wait()
    cos, sin = trig_pair(start_ref[...], me * ticks, n, ticks, ticks * n)
    (cos_high, cos_low), (sin_high, sin_low) = split(cos), split(sin)
    high_rows = jnp.concatenate([cos_high, sin_high], 0)
    all_rows = jnp.concatenate([cos_high, sin_high, cos_low, sin_low], 0)
    pl.semaphore_wait(barrier, n - 1)

    def send_comp(offset):
        pltpu.make_async_remote_copy(
            src_ref=comp_out, dst_ref=comp_in.at[offset - 1],
            send_sem=comp_send, recv_sem=comp_recv,
            device_id={"ma": peer(offset)}, device_id_type=MESH,
        ).start()

    peers(send_comp)

    vis_copy.wait()
    rows = 2 * tiles
    for tile in range(tiles):
        parts = [vis[pl.ds(2 * tile + c, ticks, stride=rows), :] for c in range(2)]
        high, low = split(jnp.concatenate(parts, 1))
        product = mul(all_rows, high)
        product = product[: 2 * n] + product[2 * n :] + mul(high_rows, low)
        real = product[:n, :LANES] + product[n:, LANES:]
        imag = product[:n, LANES:] - product[n:, :LANES]
        spec_out[:, tile, :] = real
        spec_out[:, tiles + tile, :] = imag

    def send_spec(offset):
        pltpu.make_async_remote_copy(
            src_ref=spec_out.at[peer(offset)], dst_ref=spec_in.at[offset - 1],
            send_sem=spec_send, recv_sem=spec_recv,
            device_id={"ma": peer(offset)}, device_id_type=MESH,
        ).start()

    peers(send_spec)

    arrived = comp_in.at[pl.ds(0, n - 1)]
    pltpu.make_async_copy(arrived, arrived, comp_recv).wait()
    fields = [comp_in[:, row, :] for row in range(3)]
    if 2 * count == LANES and n % 2 == 0:
        fields = [jnp.concatenate([f[: n // 2, :count], f[n // 2 :, :count]], 1) for f in fields]
    index = fields[0] - me * width
    blocks = width // LANES
    row_id = lax.broadcasted_iota(jnp.int32, (2 * blocks, LANES), 0)
    low_id = lax.broadcasted_iota(jnp.int32, (LANES, LANES), 0)
    weights, places = [], []
    for chunk in range(index.shape[0]):
        at = index[chunk : chunk + 1]
        amp = jnp.where(
            (row_id & 1) == 1, fields[2][chunk : chunk + 1], fields[1][chunk : chunk + 1]
        )
        amp = jnp.where((at >> 7) == (row_id >> 1), amp, 0)
        halves = jnp.concatenate([amp >> 6, amp & 63], 0)
        weights.append(halves.astype(F32).astype(BF16))
        places.append(jnp.where((at & 127) == low_id, 1.0, 0.0).astype(BF16))
    halves = mul(jnp.concatenate(weights, 1), jnp.concatenate(places, 1), ((1,), (1,)))
    halves = halves.astype(jnp.int32)
    summed = halves[: 2 * blocks] * 64 + halves[2 * blocks :]
    model = summed.astype(F32) * (1.0 / 1024.0)
    model = jnp.concatenate([model[2 * i : 2 * i + 2] for i in range(blocks)], 1).astype(BF16)

    transfer_copy.wait()
    lines = tiles * LANES
    predicted = mul(model, transfer[...], ((1,), (1,)))
    pred_real = predicted[0:1, :lines] - predicted[1:2, lines:]
    pred_imag = predicted[1:2, :lines] + predicted[0:1, lines:]

    spec_in[n - 1] = spec_out[me]
    arrived = spec_in.at[pl.ds(0, n - 1)]
    pltpu.make_async_copy(arrived, arrived, spec_recv).wait()
    spectra = jnp.sum(spec_in[...], 0) * (1.0 / math.sqrt(ticks * n))
    real = jnp.concatenate([spectra[i : i + 1] for i in range(tiles)], 1)
    imag = jnp.concatenate([spectra[tiles + i : tiles + i + 1] for i in range(tiles)], 1)
    real, imag = real - pred_real, imag - pred_imag
    resid = jnp.concatenate(
        [jnp.concatenate([real, imag], 1), jnp.concatenate([imag, -real], 1)], 0
    ).astype(BF16)
    alm = mul(resid, transfer[...])
    for block in range(blocks):
        out_ref[2 * block : 2 * block + 2, :] = alm[:, block * LANES : (block + 1) * LANES]

    for buffer, sem in ((comp_in, comp_send), (spec_in, spec_send)):
        sent = buffer.at[pl.ds(0, n - 1)]
        pltpu.make_async_copy(sent, sent, sem).wait()


def body(vis, transfer, band_start, comp_index, comp_amp):
    n = lax.axis_size("ma")
    ticks, _, lines = vis.shape
    m_local, _, _, width = transfer.shape
    count = comp_index.shape[0]
    tiles = lines // LANES
    blocks = width // LANES
    assert m_local == 1 and lines % LANES == 0 and width % LANES == 0 and count <= LANES
    assert (ticks * n) & (ticks * n - 1) == 0
    flat_vis = (
        vis.reshape(ticks, 2, tiles, LANES).transpose(0, 2, 1, 3).reshape(ticks * 2 * tiles, LANES)
    )
    out = pl.pallas_call(
        functools.partial(kernel, n, ticks, tiles, count, width),
        out_shape=jax.ShapeDtypeStruct((2 * blocks, LANES), F32),
        in_specs=[
            pl.BlockSpec(memory_space=pltpu.HBM),
        ]
        * 5,
        out_specs=pl.BlockSpec(memory_space=pltpu.VMEM),
        scratch_shapes=[
            pltpu.VMEM(flat_vis.shape, F32),
            pltpu.VMEM((2 * lines, width), BF16),
            pltpu.VMEM((1, 1), jnp.int32),
            pltpu.VMEM((1, count), jnp.int32),
            pltpu.VMEM((2, count), jnp.int32),
            pltpu.VMEM((4, LANES), jnp.int32),
            pltpu.VMEM((n, 4, LANES), jnp.int32),
            pltpu.VMEM((n, 2 * tiles, LANES), F32),
            pltpu.VMEM((n, 2 * tiles, LANES), F32),
        ]
        + [pltpu.SemaphoreType.DMA] * 9,
        compiler_params=pltpu.CompilerParams(
            collective_id=0, has_side_effects=True, vmem_limit_bytes=64 * 1024 * 1024
        ),
        cost_estimate=pl.CostEstimate(
            flops=2 * 2 * n * ticks * 2 * lines + 8 * lines * width * 2,
            bytes_accessed=vis.size * 4 + transfer.size * 2,
            transcendentals=0,
        ),
    )(
        flat_vis,
        transfer.reshape(2 * lines, width),
        band_start.reshape(1, 1),
        comp_index.reshape(1, count),
        comp_amp.T,
    )
    return out.reshape(blocks, 2, LANES).transpose(1, 0, 2).reshape(1, 2, width)


def solution(mesh):
    in_specs = (
        P(("grp", "ma"), None, None),
        P(("grp", "ma"), None, None, None),
        P("grp"),
        P(("grp", "ma")),
        P(("grp", "ma"), None),
    )
    out_specs = P(("grp", "ma"), None, None)
    return jax.shard_map(body, mesh=mesh, in_specs=in_specs, out_specs=out_specs, check_vma=False)
```

```python
import functools
import math

import jax
import jax.numpy as jnp
from jax import lax
from jax.experimental import pallas as pl
from jax.experimental.pallas import tpu as pltpu
from jax.sharding import PartitionSpec as P

LANES = 128
F32 = jnp.float32
BF16 = jnp.bfloat16
MESH = pl.DeviceIdType.MESH


def trig_pair(order_start, tick_start, modes, ticks, period):
    order = order_start + lax.broadcasted_iota(jnp.int32, (modes, ticks), 0)
    tick = tick_start + lax.broadcasted_iota(jnp.int32, (modes, ticks), 1)
    phase = (order * tick) & (period - 1)
    quarter = period // 4
    shift = quarter.bit_length() - 1
    quadrant = (phase + quarter // 2) >> shift
    x = (phase - (quadrant << shift)).astype(F32) * (2.0 * math.pi / period)
    z = x * x
    sin_x = x * (1.0 + z * (-1.0 / 6 + z * (1.0 / 120 + z * (-1.0 / 5040 + z * (1.0 / 362880)))))
    cos_x = 1.0 + z * (-0.5 + z * (1.0 / 24 + z * (-1.0 / 720 + z * (1.0 / 40320))))
    swap = (quadrant & 1) == 1
    cos = jnp.where(swap, sin_x, cos_x)
    sin = jnp.where(swap, cos_x, sin_x)
    cos = jnp.where(((quadrant + 1) & 2) == 2, -cos, cos)
    sin = jnp.where((quadrant & 2) == 2, -sin, sin)
    return cos, sin


def split(values):
    high = values.astype(BF16)
    return high, (values - high.astype(F32)).astype(BF16)


def mul(a, b, contract=((1,), (0,))):
    return lax.dot_general(a, b, (contract, ((), ())), preferred_element_type=F32)


def kernel(
    n, ticks, tiles, count, width,
    start_ref, vis_hbm, transfer_hbm, index_hbm, amp_hbm, out_ref,
    vis, transfer, index_ref, amp_ref, comp_out, comp_in, spec_out, spec_in,
    vis_sem, transfer_sem, index_sem, amp_sem,
    comp_send, comp_recv, spec_send, spec_recv,
):
    me = lax.axis_index("ma")
    index_copy = pltpu.make_async_copy(index_hbm, index_ref, index_sem)
    amp_copy = pltpu.make_async_copy(amp_hbm, amp_ref, amp_sem)
    vis_copy = pltpu.make_async_copy(vis_hbm, vis, vis_sem)
    transfer_copy = pltpu.make_async_copy(transfer_hbm, transfer, transfer_sem)
    for copy in (index_copy, amp_copy, vis_copy, transfer_copy):
        copy.start()

    def peers(step):
        if n <= 32:
            for offset in range(1, n):
                step(offset)
        else:
            pl.loop(1, n)(step)

    def peer(offset):
        target = me + offset
        return jnp.where(target >= n, target - n, target)

    barrier = pltpu.get_barrier_semaphore()

    def greet(offset):
        pl.semaphore_signal(barrier, inc=1, device_id={"ma": peer(offset)}, device_id_type=MESH)

    peers(greet)

    comp_out[...] = jnp.full(comp_out.shape, -1, jnp.int32)
    index_copy.wait()
    amp_copy.wait()
    comp_out[0:1, 0:count] = index_ref[...]
    comp_out[1:3, 0:count] = amp_ref[...]
    comp_in[n - 1] = comp_out[...]
    cos, sin = trig_pair(start_ref[0], me * ticks, n, ticks, ticks * n)
    (cos_high, cos_low), (sin_high, sin_low) = split(cos), split(sin)
    high_rows = jnp.concatenate([cos_high, sin_high], 0)
    all_rows = jnp.concatenate([cos_high, sin_high, cos_low, sin_low], 0)
    pl.semaphore_wait(barrier, n - 1)

    def send_comp(offset):
        pltpu.make_async_remote_copy(
            src_ref=comp_out, dst_ref=comp_in.at[offset - 1],
            send_sem=comp_send, recv_sem=comp_recv,
            device_id={"ma": peer(offset)}, device_id_type=MESH,
        ).start()

    peers(send_comp)

    vis_copy.wait()
    rows = 2 * tiles
    for tile in range(tiles):
        parts = [vis[pl.ds(2 * tile + c, ticks, stride=rows), :] for c in range(2)]
        high, low = split(jnp.concatenate(parts, 1))
        product = mul(all_rows, high)
        product = product[: 2 * n] + product[2 * n :] + mul(high_rows, low)
        real = product[:n, :LANES] + product[n:, LANES:]
        imag = product[:n, LANES:] - product[n:, :LANES]
        spec_out[:, tile, :] = real
        spec_out[:, tiles + tile, :] = imag

    def send_spec(offset):
        pltpu.make_async_remote_copy(
            src_ref=spec_out.at[peer(offset)], dst_ref=spec_in.at[offset - 1],
            send_sem=spec_send, recv_sem=spec_recv,
            device_id={"ma": peer(offset)}, device_id_type=MESH,
        ).start()

    peers(send_spec)

    arrived = comp_in.at[pl.ds(0, n - 1)]
    pltpu.make_async_copy(arrived, arrived, comp_recv).wait()
    fields = [comp_in[:, row, :] for row in range(3)]
    if 2 * count == LANES and n % 2 == 0:
        fields = [jnp.concatenate([f[: n // 2, :count], f[n // 2 :, :count]], 1) for f in fields]
    index = fields[0] - me * width
    blocks = width // LANES
    row_id = lax.broadcasted_iota(jnp.int32, (2 * blocks, LANES), 0)
    low_id = lax.broadcasted_iota(jnp.int32, (LANES, LANES), 0)
    weights, places = [], []
    for chunk in range(index.shape[0]):
        at = index[chunk : chunk + 1]
        amp = jnp.where(
            (row_id & 1) == 1, fields[2][chunk : chunk + 1], fields[1][chunk : chunk + 1]
        )
        amp = jnp.where((at >> 7) == (row_id >> 1), amp, 0)
        halves = jnp.concatenate([amp >> 6, amp & 63], 0)
        weights.append(halves.astype(F32).astype(BF16))
        places.append(jnp.where((at & 127) == low_id, 1.0, 0.0).astype(BF16))
    halves = mul(jnp.concatenate(weights, 1), jnp.concatenate(places, 1), ((1,), (1,)))
    halves = halves.astype(jnp.int32)
    summed = halves[: 2 * blocks] * 64 + halves[2 * blocks :]
    model = summed.astype(F32) * (1.0 / 1024.0)
    model = jnp.concatenate([model[2 * i : 2 * i + 2] for i in range(blocks)], 1).astype(BF16)

    transfer_copy.wait()
    lines = tiles * LANES
    predicted = mul(model, transfer[...], ((1,), (1,)))
    pred_real = predicted[0:1, :lines] - predicted[1:2, lines:]
    pred_imag = predicted[1:2, :lines] + predicted[0:1, lines:]

    spec_in[n - 1] = spec_out[me]
    arrived = spec_in.at[pl.ds(0, n - 1)]
    pltpu.make_async_copy(arrived, arrived, spec_recv).wait()
    spectra = jnp.sum(spec_in[...], 0) * (1.0 / math.sqrt(ticks * n))
    real = jnp.concatenate([spectra[i : i + 1] for i in range(tiles)], 1)
    imag = jnp.concatenate([spectra[tiles + i : tiles + i + 1] for i in range(tiles)], 1)
    real, imag = real - pred_real, imag - pred_imag
    resid = jnp.concatenate(
        [jnp.concatenate([real, imag], 1), jnp.concatenate([imag, -real], 1)], 0
    ).astype(BF16)
    alm = mul(resid, transfer[...])
    for block in range(blocks):
        out_ref[2 * block : 2 * block + 2, :] = alm[:, block * LANES : (block + 1) * LANES]

    for buffer, sem in ((comp_in, comp_send), (spec_in, spec_send)):
        sent = buffer.at[pl.ds(0, n - 1)]
        pltpu.make_async_copy(sent, sent, sem).wait()


def body(vis, transfer, band_start, comp_index, comp_amp):
    n = lax.axis_size("ma")
    ticks, _, lines = vis.shape
    m_local, _, _, width = transfer.shape
    count = comp_index.shape[0]
    tiles = lines // LANES
    blocks = width // LANES
    assert m_local == 1 and lines % LANES == 0 and width % LANES == 0 and count <= LANES
    assert (ticks * n) & (ticks * n - 1) == 0
    flat_vis = (
        vis.reshape(ticks, 2, tiles, LANES).transpose(0, 2, 1, 3).reshape(ticks * 2 * tiles, LANES)
    )
    out = pl.pallas_call(
        functools.partial(kernel, n, ticks, tiles, count, width),
        out_shape=pltpu.VMEM((2 * blocks, LANES), F32),
        in_specs=[
            pl.BlockSpec(memory_space=pltpu.SMEM),
        ]
        + [pl.BlockSpec(memory_space=pltpu.HBM)] * 4,
        out_specs=pl.BlockSpec(memory_space=pltpu.VMEM),
        scratch_shapes=[
            pltpu.VMEM(flat_vis.shape, F32),
            pltpu.VMEM((2 * lines, width), BF16),
            pltpu.VMEM((1, count), jnp.int32),
            pltpu.VMEM((2, count), jnp.int32),
            pltpu.VMEM((4, LANES), jnp.int32),
            pltpu.VMEM((n, 4, LANES), jnp.int32),
            pltpu.VMEM((n, 2 * tiles, LANES), F32),
            pltpu.VMEM((n, 2 * tiles, LANES), F32),
        ]
        + [pltpu.SemaphoreType.DMA] * 8,
        compiler_params=pltpu.CompilerParams(
            collective_id=0, has_side_effects=True, vmem_limit_bytes=40 * 1024 * 1024
        ),
        cost_estimate=pl.CostEstimate(
            flops=2 * 2 * n * ticks * 2 * lines + 8 * lines * width * 2,
            bytes_accessed=vis.size * 4 + transfer.size * 2,
            transcendentals=0,
        ),
    )(
        band_start,
        *(
            pltpu.with_memory_space_constraint(operand, pltpu.HBM)
            for operand in (
                flat_vis,
                transfer.reshape(2 * lines, width),
                comp_index.reshape(1, count),
                comp_amp.T,
            )
        ),
    )
    return out.reshape(blocks, 2, LANES).transpose(1, 0, 2).reshape(1, 2, width)


def solution(mesh):
    in_specs = (
        P(("grp", "ma"), None, None),
        P(("grp", "ma"), None, None, None),
        P("grp"),
        P(("grp", "ma")),
        P(("grp", "ma"), None),
    )
    out_specs = P(("grp", "ma"), None, None)
    return jax.shard_map(body, mesh=mesh, in_specs=in_specs, out_specs=out_specs, check_vma=False)
```

```python
import functools
import math

import jax
import jax.numpy as jnp
from jax import lax
from jax.experimental import pallas as pl
from jax.experimental.pallas import tpu as pltpu
from jax.sharding import PartitionSpec as P

LANES = 128
F32 = jnp.float32
BF16 = jnp.bfloat16
MESH = pl.DeviceIdType.MESH


def trig_pair(order_start, tick_start, modes, ticks, period):
    order = order_start + lax.broadcasted_iota(jnp.int32, (modes, ticks), 0)
    tick = tick_start + lax.broadcasted_iota(jnp.int32, (modes, ticks), 1)
    phase = (order * tick) & (period - 1)
    quarter = period // 4
    shift = quarter.bit_length() - 1
    quadrant = (phase + quarter // 2) >> shift
    x = (phase - (quadrant << shift)).astype(F32) * (2.0 * math.pi / period)
    z = x * x
    sin_x = x * (1.0 + z * (-1.0 / 6 + z * (1.0 / 120 + z * (-1.0 / 5040 + z * (1.0 / 362880)))))
    cos_x = 1.0 + z * (-0.5 + z * (1.0 / 24 + z * (-1.0 / 720 + z * (1.0 / 40320))))
    swap = (quadrant & 1) == 1
    cos = jnp.where(swap, sin_x, cos_x)
    sin = jnp.where(swap, cos_x, sin_x)
    cos = jnp.where(((quadrant + 1) & 2) == 2, -cos, cos)
    sin = jnp.where((quadrant & 2) == 2, -sin, sin)
    return cos, sin


def split(values):
    high = values.astype(BF16)
    return high, (values - high.astype(F32)).astype(BF16)


def mul(a, b, contract=((1,), (0,))):
    return lax.dot_general(a, b, (contract, ((), ())), preferred_element_type=F32)


def kernel(
    n, ticks, tiles, count, width, rows, pieces,
    start_ref, vis_hbm, transfer_hbm, index_hbm, amp_hbm, out_ref,
    vis, transfer, index_ref, amp_ref, outgoing, incoming,
    vis_sem, transfer_sem, index_sem, amp_sem, send_sem, recv_sem,
):
    me = lax.axis_index("ma")
    spec_rows = 2 * tiles
    index_copy = pltpu.make_async_copy(index_hbm, index_ref, index_sem)
    amp_copy = pltpu.make_async_copy(amp_hbm, amp_ref, amp_sem)
    piece = ticks * spec_rows // pieces
    vis_copies = []
    for i in range(pieces):
        part = pl.ds(i * piece, piece)
        vis_copies.append(pltpu.make_async_copy(vis_hbm.at[part], vis.at[part], vis_sem.at[i]))
    transfer_copy = pltpu.make_async_copy(transfer_hbm, transfer, transfer_sem)
    for copy in (*vis_copies, index_copy, amp_copy, transfer_copy):
        copy.start()

    def peers(step):
        if n <= 32:
            for offset in range(1, n):
                step(offset)
        else:
            pl.loop(1, n)(step)

    def peer(offset):
        target = me + offset
        return jnp.where(target >= n, target - n, target)

    def slot(index):
        return pl.ds(pl.multiple_of(index * rows, rows), rows)

    barrier = pltpu.get_barrier_semaphore()

    def greet(offset):
        pl.semaphore_signal(barrier, inc=1, device_id={"ma": peer(offset)}, device_id_type=MESH)

    peers(greet)

    cos, sin = trig_pair(start_ref[0], me * ticks, n, ticks, ticks * n)
    (cos_high, cos_low), (sin_high, sin_low) = split(cos), split(sin)
    high_rows = jnp.concatenate([cos_high, sin_high], 0)
    all_rows = jnp.concatenate([cos_high, sin_high, cos_low, sin_low], 0)

    index_copy.wait()
    amp_copy.wait()
    fields = [index_ref[...], amp_ref[0:1], amp_ref[1:2]]
    for row in range(spec_rows, rows):
        if row < spec_rows + 3:
            field = fields[row - spec_rows].astype(F32)
            if count < LANES:
                field = jnp.concatenate([field, jnp.full((1, LANES - count), -1.0, F32)], 1)
        else:
            field = jnp.zeros((1, LANES), F32)
        outgoing[pl.ds(row, n, stride=rows), :] = jnp.broadcast_to(field, (n, LANES))

    for copy in vis_copies:
        copy.wait()
    for tile in range(tiles):
        parts = [vis[pl.ds(2 * tile + c, ticks, stride=spec_rows), :] for c in range(2)]
        high, low = split(jnp.concatenate(parts, 1))
        product = mul(all_rows, high)
        product = product[: 2 * n] + product[2 * n :] + mul(high_rows, low)
        real = product[:n, :LANES] + product[n:, LANES:]
        imag = product[:n, LANES:] - product[n:, :LANES]
        outgoing[pl.ds(tile, n, stride=rows), :] = real
        outgoing[pl.ds(tiles + tile, n, stride=rows), :] = imag

    pl.semaphore_wait(barrier, n - 1)

    def send(offset):
        pltpu.make_async_remote_copy(
            src_ref=outgoing.at[slot(peer(offset))], dst_ref=incoming.at[slot(offset - 1)],
            send_sem=send_sem, recv_sem=recv_sem,
            device_id={"ma": peer(offset)}, device_id_type=MESH,
        ).start()

    peers(send)
    incoming[slot(n - 1), :] = outgoing[slot(me), :]
    transfer_copy.wait()
    arrived = incoming.at[pl.ds(0, (n - 1) * rows)]
    pltpu.make_async_copy(arrived, arrived, recv_sem).wait()

    fields = [
        incoming[pl.ds(spec_rows + row, n, stride=rows), :].astype(jnp.int32) for row in range(3)
    ]
    if 2 * count == LANES and n % 2 == 0:
        fields = [jnp.concatenate([f[: n // 2, :count], f[n // 2 :, :count]], 1) for f in fields]
    index = fields[0] - me * width
    blocks = width // LANES
    row_id = lax.broadcasted_iota(jnp.int32, (2 * blocks, LANES), 0)
    low_id = lax.broadcasted_iota(jnp.int32, (LANES, LANES), 0)
    weights, places = [], []
    for chunk in range(index.shape[0]):
        at = index[chunk : chunk + 1]
        amp = jnp.where(
            (row_id & 1) == 1, fields[2][chunk : chunk + 1], fields[1][chunk : chunk + 1]
        )
        amp = jnp.where((at >> 7) == (row_id >> 1), amp, 0)
        halves = jnp.concatenate([amp >> 6, amp & 63], 0)
        weights.append(halves.astype(F32).astype(BF16))
        places.append(jnp.where((at & 127) == low_id, 1.0, 0.0).astype(BF16))
    halves = mul(jnp.concatenate(weights, 1), jnp.concatenate(places, 1), ((1,), (1,)))
    halves = halves.astype(jnp.int32)
    summed = halves[: 2 * blocks] * 64 + halves[2 * blocks :]
    model = summed.astype(F32) * (1.0 / 1024.0)
    model = jnp.concatenate([model[2 * i : 2 * i + 2] for i in range(blocks)], 1).astype(BF16)

    lines = tiles * LANES
    predicted = mul(model, transfer[...], ((1,), (1,)))
    pred_real = predicted[0:1, :lines] - predicted[1:2, lines:]
    pred_imag = predicted[1:2, :lines] + predicted[0:1, lines:]

    spectra = jnp.sum(incoming[...].reshape(n, rows, LANES), 0) * (1.0 / math.sqrt(ticks * n))
    real = jnp.concatenate([spectra[i : i + 1] for i in range(tiles)], 1)
    imag = jnp.concatenate([spectra[tiles + i : tiles + i + 1] for i in range(tiles)], 1)
    real, imag = real - pred_real, imag - pred_imag
    resid = jnp.concatenate(
        [jnp.concatenate([real, imag], 1), jnp.concatenate([imag, -real], 1)], 0
    ).astype(BF16)
    alm = mul(resid, transfer[...])
    for block in range(blocks):
        out_ref[2 * block : 2 * block + 2, :] = alm[:, block * LANES : (block + 1) * LANES]

    pltpu.make_async_copy(arrived, arrived, send_sem).wait()


def body(vis, transfer, band_start, comp_index, comp_amp):
    n = lax.axis_size("ma")
    ticks, _, lines = vis.shape
    m_local, _, _, width = transfer.shape
    count = comp_index.shape[0]
    tiles = lines // LANES
    blocks = width // LANES
    assert m_local == 1 and lines % LANES == 0 and width % LANES == 0 and count <= LANES
    rows = -(-(2 * tiles + 3) // 8) * 8
    pieces = 4
    assert ticks * 2 * tiles % (8 * pieces) == 0
    assert (ticks * n) & (ticks * n - 1) == 0
    flat_vis = (
        vis.reshape(ticks, 2, tiles, LANES).transpose(0, 2, 1, 3).reshape(ticks * 2 * tiles, LANES)
    )
    out = pl.pallas_call(
        functools.partial(kernel, n, ticks, tiles, count, width, rows, pieces),
        out_shape=pltpu.VMEM((2 * blocks, LANES), F32),
        in_specs=[
            pl.BlockSpec(memory_space=pltpu.SMEM),
        ]
        + [pl.BlockSpec(memory_space=pltpu.HBM)] * 4,
        out_specs=pl.BlockSpec(memory_space=pltpu.VMEM),
        scratch_shapes=[
            pltpu.VMEM(flat_vis.shape, F32),
            pltpu.VMEM((2 * lines, width), BF16),
            pltpu.VMEM((1, count), jnp.int32),
            pltpu.VMEM((2, count), jnp.int32),
            pltpu.VMEM((n * rows, LANES), F32),
            pltpu.VMEM((n * rows, LANES), F32),
            pltpu.SemaphoreType.DMA((pieces,)),
        ]
        + [pltpu.SemaphoreType.DMA] * 5,
        compiler_params=pltpu.CompilerParams(
            collective_id=0, has_side_effects=True, vmem_limit_bytes=40 * 1024 * 1024
        ),
        cost_estimate=pl.CostEstimate(
            flops=2 * 2 * n * ticks * 2 * lines + 8 * lines * width * 2,
            bytes_accessed=vis.size * 4 + transfer.size * 2,
            transcendentals=0,
        ),
    )(
        band_start,
        *(
            pltpu.with_memory_space_constraint(operand, pltpu.HBM)
            for operand in (
                flat_vis,
                transfer.reshape(2 * lines, width),
                comp_index.reshape(1, count),
                comp_amp.T,
            )
        ),
    )
    return out.reshape(blocks, 2, LANES).transpose(1, 0, 2).reshape(1, 2, width)


def solution(mesh):
    in_specs = (
        P(("grp", "ma"), None, None),
        P(("grp", "ma"), None, None, None),
        P("grp"),
        P(("grp", "ma")),
        P(("grp", "ma"), None),
    )
    out_specs = P(("grp", "ma"), None, None)
    return jax.shard_map(body, mesh=mesh, in_specs=in_specs, out_specs=out_specs, check_vma=False)
```

```python
import functools
import math

import jax
import jax.numpy as jnp
from jax import lax
from jax.experimental import pallas as pl
from jax.experimental.pallas import tpu as pltpu
from jax.sharding import PartitionSpec as P

LANES = 128
F32 = jnp.float32
BF16 = jnp.bfloat16
MESH = pl.DeviceIdType.MESH


def trig_pair(order_start, tick_start, modes, ticks, period):
    order = order_start + lax.broadcasted_iota(jnp.int32, (modes, ticks), 0)
    tick = tick_start + lax.broadcasted_iota(jnp.int32, (modes, ticks), 1)
    phase = (order * tick) & (period - 1)
    quarter = period // 4
    shift = quarter.bit_length() - 1
    quadrant = (phase + quarter // 2) >> shift
    x = (phase - (quadrant << shift)).astype(F32) * (2.0 * math.pi / period)
    z = x * x
    sin_x = x * (1.0 + z * (-1.0 / 6 + z * (1.0 / 120 + z * (-1.0 / 5040 + z * (1.0 / 362880)))))
    cos_x = 1.0 + z * (-0.5 + z * (1.0 / 24 + z * (-1.0 / 720 + z * (1.0 / 40320))))
    swap = (quadrant & 1) == 1
    cos = jnp.where(swap, sin_x, cos_x)
    sin = jnp.where(swap, cos_x, sin_x)
    cos = jnp.where(((quadrant + 1) & 2) == 2, -cos, cos)
    sin = jnp.where((quadrant & 2) == 2, -sin, sin)
    return cos, sin


def split(values):
    high = values.astype(BF16)
    return high, (values - high.astype(F32)).astype(BF16)


def mul(a, b, contract=((1,), (0,))):
    return lax.dot_general(a, b, (contract, ((), ())), preferred_element_type=F32)


def kernel(
    n, ticks, tiles, count, width, pieces,
    start_ref, vis_hbm, transfer_hbm, index_hbm, amp_hbm, out_ref,
    vis, transfer, index_ref, amp_ref, comp_out, comp_in, spec_out, spec_in,
    vis_sem, transfer_sem, index_sem, amp_sem,
    comp_send, comp_recv, spec_send, spec_recv,
):
    me = lax.axis_index("ma")
    index_copy = pltpu.make_async_copy(index_hbm, index_ref, index_sem)
    amp_copy = pltpu.make_async_copy(amp_hbm, amp_ref, amp_sem)
    piece = vis.shape[0] // pieces
    vis_copies = []
    for i in range(pieces):
        part = pl.ds(i * piece, piece)
        vis_copies.append(pltpu.make_async_copy(vis_hbm.at[part], vis.at[part], vis_sem.at[i]))
    transfer_copy = pltpu.make_async_copy(transfer_hbm, transfer, transfer_sem)
    for copy in (*vis_copies, index_copy, amp_copy, transfer_copy):
        copy.start()

    def peers(step):
        if n <= 32:
            for offset in range(1, n):
                step(offset)
        else:
            pl.loop(1, n)(step)

    def peer(offset):
        target = me + offset
        return jnp.where(target >= n, target - n, target)

    barrier = pltpu.get_barrier_semaphore()

    def greet(offset):
        pl.semaphore_signal(barrier, inc=1, device_id={"ma": peer(offset)}, device_id_type=MESH)

    peers(greet)

    comp_out[...] = jnp.full(comp_out.shape, -1, jnp.int32)
    index_copy.wait()
    amp_copy.wait()
    comp_out[0:1, 0:count] = index_ref[...]
    comp_out[1:3, 0:count] = amp_ref[...]
    comp_in[n - 1] = comp_out[...]
    cos, sin = trig_pair(start_ref[0], me * ticks, n, ticks, ticks * n)
    (cos_high, cos_low), (sin_high, sin_low) = split(cos), split(sin)
    high_rows = jnp.concatenate([cos_high, sin_high], 0)
    all_rows = jnp.concatenate([cos_high, sin_high, cos_low, sin_low], 0)
    for copy in vis_copies:
        copy.wait()
    rows = 2 * tiles
    for tile in range(tiles):
        parts = [vis[pl.ds(2 * tile + c, ticks, stride=rows), :] for c in range(2)]
        high, low = split(jnp.concatenate(parts, 1))
        product = mul(all_rows, high)
        product = product[: 2 * n] + product[2 * n :] + mul(high_rows, low)
        real = product[:n, :LANES] + product[n:, LANES:]
        imag = product[:n, LANES:] - product[n:, :LANES]
        spec_out[:, tile, :] = real
        spec_out[:, tiles + tile, :] = imag

    pl.semaphore_wait(barrier, n - 1)

    def send_comp(offset):
        pltpu.make_async_remote_copy(
            src_ref=comp_out, dst_ref=comp_in.at[offset - 1],
            send_sem=comp_send, recv_sem=comp_recv,
            device_id={"ma": peer(offset)}, device_id_type=MESH,
        ).start()

    peers(send_comp)

    def send_spec(offset):
        pltpu.make_async_remote_copy(
            src_ref=spec_out.at[peer(offset)], dst_ref=spec_in.at[offset - 1],
            send_sem=spec_send, recv_sem=spec_recv,
            device_id={"ma": peer(offset)}, device_id_type=MESH,
        ).start()

    peers(send_spec)

    arrived = comp_in.at[pl.ds(0, n - 1)]
    pltpu.make_async_copy(arrived, arrived, comp_recv).wait()
    fields = [comp_in[:, row, :] for row in range(3)]
    if 2 * count == LANES and n % 2 == 0:
        fields = [jnp.concatenate([f[: n // 2, :count], f[n // 2 :, :count]], 1) for f in fields]
    index = fields[0] - me * width
    blocks = width // LANES
    row_id = lax.broadcasted_iota(jnp.int32, (2 * blocks, LANES), 0)
    low_id = lax.broadcasted_iota(jnp.int32, (LANES, LANES), 0)
    weights, places = [], []
    for chunk in range(index.shape[0]):
        at = index[chunk : chunk + 1]
        amp = jnp.where(
            (row_id & 1) == 1, fields[2][chunk : chunk + 1], fields[1][chunk : chunk + 1]
        )
        amp = jnp.where((at >> 7) == (row_id >> 1), amp, 0)
        halves = jnp.concatenate([amp >> 6, amp & 63], 0)
        weights.append(halves.astype(F32).astype(BF16))
        places.append(jnp.where((at & 127) == low_id, 1.0, 0.0).astype(BF16))
    halves = mul(jnp.concatenate(weights, 1), jnp.concatenate(places, 1), ((1,), (1,)))
    halves = halves.astype(jnp.int32)
    summed = halves[: 2 * blocks] * 64 + halves[2 * blocks :]
    model = summed.astype(F32) * (1.0 / 1024.0)
    model = jnp.concatenate([model[2 * i : 2 * i + 2] for i in range(blocks)], 1).astype(BF16)

    transfer_copy.wait()
    lines = tiles * LANES
    predicted = mul(model, transfer[...], ((1,), (1,)))
    pred_real = predicted[0:1, :lines] - predicted[1:2, lines:]
    pred_imag = predicted[1:2, :lines] + predicted[0:1, lines:]

    spec_in[n - 1] = spec_out[me]
    arrived = spec_in.at[pl.ds(0, n - 1)]
    pltpu.make_async_copy(arrived, arrived, spec_recv).wait()
    spectra = jnp.sum(spec_in[...], 0) * (1.0 / math.sqrt(ticks * n))
    real = jnp.concatenate([spectra[i : i + 1] for i in range(tiles)], 1)
    imag = jnp.concatenate([spectra[tiles + i : tiles + i + 1] for i in range(tiles)], 1)
    real, imag = real - pred_real, imag - pred_imag
    resid = jnp.concatenate(
        [jnp.concatenate([real, imag], 1), jnp.concatenate([imag, -real], 1)], 0
    ).astype(BF16)
    alm = mul(resid, transfer[...])
    for block in range(blocks):
        out_ref[2 * block : 2 * block + 2, :] = alm[:, block * LANES : (block + 1) * LANES]

    for buffer, sem in ((comp_in, comp_send), (spec_in, spec_send)):
        sent = buffer.at[pl.ds(0, n - 1)]
        pltpu.make_async_copy(sent, sent, sem).wait()


def body(vis, transfer, band_start, comp_index, comp_amp):
    n = lax.axis_size("ma")
    ticks, _, lines = vis.shape
    m_local, _, _, width = transfer.shape
    count = comp_index.shape[0]
    tiles = lines // LANES
    blocks = width // LANES
    assert m_local == 1 and lines % LANES == 0 and width % LANES == 0 and count <= LANES
    pieces = 4
    assert ticks * 2 * tiles % (8 * pieces) == 0
    assert (ticks * n) & (ticks * n - 1) == 0
    flat_vis = (
        vis.reshape(ticks, 2, tiles, LANES).transpose(0, 2, 1, 3).reshape(ticks * 2 * tiles, LANES)
    )
    out = pl.pallas_call(
        functools.partial(kernel, n, ticks, tiles, count, width, pieces),
        out_shape=pltpu.VMEM((2 * blocks, LANES), F32),
        in_specs=[
            pl.BlockSpec(memory_space=pltpu.SMEM),
        ]
        + [pl.BlockSpec(memory_space=pltpu.HBM)] * 4,
        out_specs=pl.BlockSpec(memory_space=pltpu.VMEM),
        scratch_shapes=[
            pltpu.VMEM(flat_vis.shape, F32),
            pltpu.VMEM((2 * lines, width), BF16),
            pltpu.VMEM((1, count), jnp.int32),
            pltpu.VMEM((2, count), jnp.int32),
            pltpu.VMEM((4, LANES), jnp.int32),
            pltpu.VMEM((n, 4, LANES), jnp.int32),
            pltpu.VMEM((n, 2 * tiles, LANES), F32),
            pltpu.VMEM((n, 2 * tiles, LANES), F32),
        ]
        + [pltpu.SemaphoreType.DMA((pieces,))]
        + [pltpu.SemaphoreType.DMA] * 7,
        compiler_params=pltpu.CompilerParams(
            collective_id=0, has_side_effects=True, vmem_limit_bytes=40 * 1024 * 1024
        ),
        cost_estimate=pl.CostEstimate(
            flops=2 * 2 * n * ticks * 2 * lines + 8 * lines * width * 2,
            bytes_accessed=vis.size * 4 + transfer.size * 2,
            transcendentals=0,
        ),
    )(
        band_start,
        *(
            pltpu.with_memory_space_constraint(operand, pltpu.HBM)
            for operand in (
                flat_vis,
                transfer.reshape(2 * lines, width),
                comp_index.reshape(1, count),
                comp_amp.T,
            )
        ),
    )
    return out.reshape(blocks, 2, LANES).transpose(1, 0, 2).reshape(1, 2, width)


def solution(mesh):
    in_specs = (
        P(("grp", "ma"), None, None),
        P(("grp", "ma"), None, None, None),
        P("grp"),
        P(("grp", "ma")),
        P(("grp", "ma"), None),
    )
    out_specs = P(("grp", "ma"), None, None)
    return jax.shard_map(body, mesh=mesh, in_specs=in_specs, out_specs=out_specs, check_vma=False)
```

```python
import functools
import math

import jax
import jax.numpy as jnp
from jax import lax
from jax.experimental import pallas as pl
from jax.experimental.pallas import tpu as pltpu
from jax.sharding import PartitionSpec as P

LANES = 128
F32 = jnp.float32
BF16 = jnp.bfloat16
MESH = pl.DeviceIdType.MESH


def trig_pair(order_start, tick_start, modes, ticks, period):
    order = order_start + lax.broadcasted_iota(jnp.int32, (modes, ticks), 0)
    tick = tick_start + lax.broadcasted_iota(jnp.int32, (modes, ticks), 1)
    phase = (order * tick) & (period - 1)
    quarter = period // 4
    shift = quarter.bit_length() - 1
    quadrant = (phase + quarter // 2) >> shift
    x = (phase - (quadrant << shift)).astype(F32) * (2.0 * math.pi / period)
    z = x * x
    sin_x = x * (1.0 + z * (-1.0 / 6 + z * (1.0 / 120 + z * (-1.0 / 5040 + z * (1.0 / 362880)))))
    cos_x = 1.0 + z * (-0.5 + z * (1.0 / 24 + z * (-1.0 / 720 + z * (1.0 / 40320))))
    swap = (quadrant & 1) == 1
    cos = jnp.where(swap, sin_x, cos_x)
    sin = jnp.where(swap, cos_x, sin_x)
    cos = jnp.where(((quadrant + 1) & 2) == 2, -cos, cos)
    sin = jnp.where((quadrant & 2) == 2, -sin, sin)
    return cos, sin


def split(values):
    high = values.astype(BF16)
    return high, (values - high.astype(F32)).astype(BF16)


def mul(a, b, contract=((1,), (0,))):
    return lax.dot_general(a, b, (contract, ((), ())), preferred_element_type=F32)


def kernel(
    n, ticks, tiles, count, width, pieces,
    start_ref, vis_hbm, transfer_hbm, index_hbm, amp_hbm, out_ref,
    vis, transfer, index_ref, amp_ref, comp_out, comp_in, spec_out, spec_in,
    vis_sem, transfer_sem, index_sem, amp_sem,
    comp_send, comp_recv, spec_send, spec_recv,
):
    me = lax.axis_index("ma")
    index_copy = pltpu.make_async_copy(index_hbm, index_ref, index_sem)
    amp_copy = pltpu.make_async_copy(amp_hbm, amp_ref, amp_sem)
    piece = vis.shape[0] // pieces
    vis_copies = []
    for i in range(pieces):
        part = pl.ds(i * piece, piece)
        vis_copies.append(pltpu.make_async_copy(vis_hbm.at[part], vis.at[part], vis_sem.at[i]))
    transfer_copy = pltpu.make_async_copy(transfer_hbm, transfer, transfer_sem)
    for copy in (index_copy, amp_copy, *vis_copies, transfer_copy):
        copy.start()

    def peers(step):
        if n <= 32:
            for offset in range(1, n):
                step(offset)
        else:
            pl.loop(1, n)(step)

    def peer(offset):
        target = me + offset
        return jnp.where(target >= n, target - n, target)

    barrier = pltpu.get_barrier_semaphore()

    def greet(offset):
        pl.semaphore_signal(barrier, inc=1, device_id={"ma": peer(offset)}, device_id_type=MESH)

    peers(greet)

    cos, sin = trig_pair(start_ref[0], me * ticks, n, ticks, ticks * n)
    (cos_high, cos_low), (sin_high, sin_low) = split(cos), split(sin)
    high_rows = jnp.concatenate([cos_high, sin_high], 0)
    all_rows = jnp.concatenate([cos_high, sin_high, cos_low, sin_low], 0)

    comp_out[...] = jnp.full(comp_out.shape, -1, jnp.int32)
    index_copy.wait()
    amp_copy.wait()
    comp_out[0:1, 0:count] = index_ref[...]
    comp_out[1:3, 0:count] = amp_ref[...]
    comp_in[n - 1] = comp_out[...]
    pl.semaphore_wait(barrier, n - 1)

    def send_comp(offset):
        pltpu.make_async_remote_copy(
            src_ref=comp_out, dst_ref=comp_in.at[offset - 1],
            send_sem=comp_send, recv_sem=comp_recv,
            device_id={"ma": peer(offset)}, device_id_type=MESH,
        ).start()

    peers(send_comp)

    for copy in vis_copies:
        copy.wait()
    rows = 2 * tiles
    for tile in range(tiles):
        parts = [vis[pl.ds(2 * tile + c, ticks, stride=rows), :] for c in range(2)]
        high, low = split(jnp.concatenate(parts, 1))
        product = mul(all_rows, high)
        product = product[: 2 * n] + product[2 * n :] + mul(high_rows, low)
        real = product[:n, :LANES] + product[n:, LANES:]
        imag = product[:n, LANES:] - product[n:, :LANES]
        spec_out[:, tile, :] = real
        spec_out[:, tiles + tile, :] = imag

    def send_spec(offset):
        pltpu.make_async_remote_copy(
            src_ref=spec_out.at[peer(offset)], dst_ref=spec_in.at[offset - 1],
            send_sem=spec_send, recv_sem=spec_recv,
            device_id={"ma": peer(offset)}, device_id_type=MESH,
        ).start()

    peers(send_spec)

    arrived = comp_in.at[pl.ds(0, n - 1)]
    pltpu.make_async_copy(arrived, arrived, comp_recv).wait()
    fields = [comp_in[:, row, :] for row in range(3)]
    if 2 * count == LANES and n % 2 == 0:
        fields = [jnp.concatenate([f[: n // 2, :count], f[n // 2 :, :count]], 1) for f in fields]
    index = fields[0] - me * width
    blocks = width // LANES
    row_id = lax.broadcasted_iota(jnp.int32, (2 * blocks, LANES), 0)
    low_id = lax.broadcasted_iota(jnp.int32, (LANES, LANES), 0)
    weights, places = [], []
    for chunk in range(index.shape[0]):
        at = index[chunk : chunk + 1]
        amp = jnp.where(
            (row_id & 1) == 1, fields[2][chunk : chunk + 1], fields[1][chunk : chunk + 1]
        )
        amp = jnp.where((at >> 7) == (row_id >> 1), amp, 0)
        halves = jnp.concatenate([amp >> 6, amp & 63], 0)
        weights.append(halves.astype(F32).astype(BF16))
        places.append(jnp.where((at & 127) == low_id, 1.0, 0.0).astype(BF16))
    halves = mul(jnp.concatenate(weights, 1), jnp.concatenate(places, 1), ((1,), (1,)))
    halves = halves.astype(jnp.int32)
    summed = halves[: 2 * blocks] * 64 + halves[2 * blocks :]
    model = summed.astype(F32) * (1.0 / 1024.0)
    model = jnp.concatenate([model[2 * i : 2 * i + 2] for i in range(blocks)], 1).astype(BF16)

    transfer_copy.wait()
    lines = tiles * LANES
    predicted = mul(model, transfer[...], ((1,), (1,)))
    pred_real = predicted[0:1, :lines] - predicted[1:2, lines:]
    pred_imag = predicted[1:2, :lines] + predicted[0:1, lines:]

    spec_in[n - 1] = spec_out[me]
    arrived = spec_in.at[pl.ds(0, n - 1)]
    pltpu.make_async_copy(arrived, arrived, spec_recv).wait()
    spectra = jnp.sum(spec_in[...], 0) * (1.0 / math.sqrt(ticks * n))
    real = jnp.concatenate([spectra[i : i + 1] for i in range(tiles)], 1)
    imag = jnp.concatenate([spectra[tiles + i : tiles + i + 1] for i in range(tiles)], 1)
    real, imag = real - pred_real, imag - pred_imag
    resid = jnp.concatenate(
        [jnp.concatenate([real, imag], 1), jnp.concatenate([imag, -real], 1)], 0
    ).astype(BF16)
    alm = mul(resid, transfer[...])
    for block in range(blocks):
        out_ref[2 * block : 2 * block + 2, :] = alm[:, block * LANES : (block + 1) * LANES]

    for buffer, sem in ((comp_in, comp_send), (spec_in, spec_send)):
        sent = buffer.at[pl.ds(0, n - 1)]
        pltpu.make_async_copy(sent, sent, sem).wait()


def body(vis, transfer, band_start, comp_index, comp_amp):
    n = lax.axis_size("ma")
    ticks, _, lines = vis.shape
    m_local, _, _, width = transfer.shape
    count = comp_index.shape[0]
    tiles = lines // LANES
    blocks = width // LANES
    assert m_local == 1 and lines % LANES == 0 and width % LANES == 0 and count <= LANES
    pieces = 4
    assert ticks * 2 * tiles % (8 * pieces) == 0
    assert (ticks * n) & (ticks * n - 1) == 0
    flat_vis = (
        vis.reshape(ticks, 2, tiles, LANES).transpose(0, 2, 1, 3).reshape(ticks * 2 * tiles, LANES)
    )
    out = pl.pallas_call(
        functools.partial(kernel, n, ticks, tiles, count, width, pieces),
        out_shape=pltpu.VMEM((2 * blocks, LANES), F32),
        in_specs=[
            pl.BlockSpec(memory_space=pltpu.SMEM),
        ]
        + [pl.BlockSpec(memory_space=pltpu.HBM)] * 4,
        out_specs=pl.BlockSpec(memory_space=pltpu.VMEM),
        scratch_shapes=[
            pltpu.VMEM(flat_vis.shape, F32),
            pltpu.VMEM((2 * lines, width), BF16),
            pltpu.VMEM((1, count), jnp.int32),
            pltpu.VMEM((2, count), jnp.int32),
            pltpu.VMEM((4, LANES), jnp.int32),
            pltpu.VMEM((n, 4, LANES), jnp.int32),
            pltpu.VMEM((n, 2 * tiles, LANES), F32),
            pltpu.VMEM((n, 2 * tiles, LANES), F32),
        ]
        + [pltpu.SemaphoreType.DMA((pieces,))]
        + [pltpu.SemaphoreType.DMA] * 7,
        compiler_params=pltpu.CompilerParams(
            collective_id=0, has_side_effects=True, vmem_limit_bytes=40 * 1024 * 1024
        ),
        cost_estimate=pl.CostEstimate(
            flops=2 * 2 * n * ticks * 2 * lines + 8 * lines * width * 2,
            bytes_accessed=vis.size * 4 + transfer.size * 2,
            transcendentals=0,
        ),
    )(
        band_start,
        *(
            pltpu.with_memory_space_constraint(operand, pltpu.HBM)
            for operand in (
                flat_vis,
                transfer.reshape(2 * lines, width),
                comp_index.reshape(1, count),
                comp_amp.T,
            )
        ),
    )
    return out.reshape(blocks, 2, LANES).transpose(1, 0, 2).reshape(1, 2, width)


def solution(mesh):
    in_specs = (
        P(("grp", "ma"), None, None),
        P(("grp", "ma"), None, None, None),
        P("grp"),
        P(("grp", "ma")),
        P(("grp", "ma"), None),
    )
    out_specs = P(("grp", "ma"), None, None)
    return jax.shard_map(body, mesh=mesh, in_specs=in_specs, out_specs=out_specs, check_vma=False)
```

```python
import functools
import math

import jax
import jax.numpy as jnp
from jax import lax
from jax.experimental import pallas as pl
from jax.experimental.pallas import tpu as pltpu
from jax.sharding import PartitionSpec as P

LANES = 128
F32 = jnp.float32
BF16 = jnp.bfloat16
MESH = pl.DeviceIdType.MESH


def trig_pair(order_start, tick_start, modes, ticks, period):
    order = order_start + lax.broadcasted_iota(jnp.int32, (modes, ticks), 0)
    tick = tick_start + lax.broadcasted_iota(jnp.int32, (modes, ticks), 1)
    phase = (order * tick) & (period - 1)
    quarter = period // 4
    shift = quarter.bit_length() - 1
    quadrant = (phase + quarter // 2) >> shift
    x = (phase - (quadrant << shift)).astype(F32) * (2.0 * math.pi / period)
    z = x * x
    sin_x = x * (1.0 + z * (-1.0 / 6 + z * (1.0 / 120 + z * (-1.0 / 5040 + z * (1.0 / 362880)))))
    cos_x = 1.0 + z * (-0.5 + z * (1.0 / 24 + z * (-1.0 / 720 + z * (1.0 / 40320))))
    swap = (quadrant & 1) == 1
    cos = jnp.where(swap, sin_x, cos_x)
    sin = jnp.where(swap, cos_x, sin_x)
    cos = jnp.where(((quadrant + 1) & 2) == 2, -cos, cos)
    sin = jnp.where((quadrant & 2) == 2, -sin, sin)
    return cos, sin


def split(values):
    high = values.astype(BF16)
    return high, (values - high.astype(F32)).astype(BF16)


def mul(a, b, contract=((1,), (0,))):
    return lax.dot_general(a, b, (contract, ((), ())), preferred_element_type=F32)


def kernel(
    n, ticks, tiles, count, width, pieces,
    start_ref, vis_hbm, transfer_hbm, index_hbm, amp_hbm, out_ref,
    vis, transfer, index_ref, amp_ref, comp_out, comp_in, spec_out, spec_in,
    vis_sem, transfer_sem, index_sem, amp_sem,
    comp_send, comp_recv, spec_send, spec_recv,
):
    me = lax.axis_index("ma")
    index_copy = pltpu.make_async_copy(index_hbm, index_ref, index_sem)
    amp_copy = pltpu.make_async_copy(amp_hbm, amp_ref, amp_sem)
    piece = vis.shape[0] // pieces
    vis_copies = []
    for i in range(pieces):
        part = pl.ds(i * piece, piece)
        vis_copies.append(pltpu.make_async_copy(vis_hbm.at[part], vis.at[part], vis_sem.at[i]))
    transfer_copy = pltpu.make_async_copy(transfer_hbm, transfer, transfer_sem)

    def peers(step):
        if n <= 32:
            for offset in range(1, n):
                step(offset)
        else:
            pl.loop(1, n)(step)

    def peer(offset):
        target = me + offset
        return jnp.where(target >= n, target - n, target)

    barrier = pltpu.get_barrier_semaphore()

    def greet(offset):
        pl.semaphore_signal(barrier, inc=1, device_id={"ma": peer(offset)}, device_id_type=MESH)

    peers(greet)
    for copy in (index_copy, amp_copy, *vis_copies, transfer_copy):
        copy.start()

    cos, sin = trig_pair(start_ref[0], me * ticks, n, ticks, ticks * n)
    (cos_high, cos_low), (sin_high, sin_low) = split(cos), split(sin)
    high_rows = jnp.concatenate([cos_high, sin_high], 0)
    all_rows = jnp.concatenate([cos_high, sin_high, cos_low, sin_low], 0)

    comp_out[...] = jnp.full(comp_out.shape, -1, jnp.int32)
    index_copy.wait()
    amp_copy.wait()
    comp_out[0:1, 0:count] = index_ref[...]
    comp_out[1:3, 0:count] = amp_ref[...]
    comp_in[n - 1] = comp_out[...]
    def transform(some_tiles):
        for tile in some_tiles:
            parts = [vis[pl.ds(2 * tile + c, ticks, stride=2 * tiles), :] for c in range(2)]
            high, low = split(jnp.concatenate(parts, 1))
            product = mul(all_rows, high)
            product = product[: 2 * n] + product[2 * n :] + mul(high_rows, low)
            real = product[:n, :LANES] + product[n:, LANES:]
            imag = product[:n, LANES:] - product[n:, :LANES]
            spec_out[:, tile, :] = real
            spec_out[:, tiles + tile, :] = imag

    for copy in vis_copies:
        copy.wait()
    transform(range(tiles // 2))
    pl.semaphore_wait(barrier, n - 1)

    def send_comp(offset):
        pltpu.make_async_remote_copy(
            src_ref=comp_out, dst_ref=comp_in.at[offset - 1],
            send_sem=comp_send, recv_sem=comp_recv,
            device_id={"ma": peer(offset)}, device_id_type=MESH,
        ).start()

    peers(send_comp)

    transform(range(tiles // 2, tiles))

    def send_spec(offset):
        pltpu.make_async_remote_copy(
            src_ref=spec_out.at[peer(offset)], dst_ref=spec_in.at[offset - 1],
            send_sem=spec_send, recv_sem=spec_recv,
            device_id={"ma": peer(offset)}, device_id_type=MESH,
        ).start()

    peers(send_spec)

    arrived = comp_in.at[pl.ds(0, n - 1)]
    pltpu.make_async_copy(arrived, arrived, comp_recv).wait()
    fields = [comp_in[:, row, :] for row in range(3)]
    if 2 * count == LANES and n % 2 == 0:
        fields = [jnp.concatenate([f[: n // 2, :count], f[n // 2 :, :count]], 1) for f in fields]
    index = fields[0] - me * width
    blocks = width // LANES
    row_id = lax.broadcasted_iota(jnp.int32, (2 * blocks, LANES), 0)
    low_id = lax.broadcasted_iota(jnp.int32, (LANES, LANES), 0)
    weights, places = [], []
    for chunk in range(index.shape[0]):
        at = index[chunk : chunk + 1]
        amp = jnp.where(
            (row_id & 1) == 1, fields[2][chunk : chunk + 1], fields[1][chunk : chunk + 1]
        )
        amp = jnp.where((at >> 7) == (row_id >> 1), amp, 0)
        halves = jnp.concatenate([amp >> 6, amp & 63], 0)
        weights.append(halves.astype(F32).astype(BF16))
        places.append(jnp.where((at & 127) == low_id, 1.0, 0.0).astype(BF16))
    halves = mul(jnp.concatenate(weights, 1), jnp.concatenate(places, 1), ((1,), (1,)))
    halves = halves.astype(jnp.int32)
    summed = halves[: 2 * blocks] * 64 + halves[2 * blocks :]
    model = summed.astype(F32) * (1.0 / 1024.0)
    model = jnp.concatenate([model[2 * i : 2 * i + 2] for i in range(blocks)], 1).astype(BF16)

    transfer_copy.wait()
    lines = tiles * LANES
    predicted = mul(model, transfer[...], ((1,), (1,)))
    pred_real = predicted[0:1, :lines] - predicted[1:2, lines:]
    pred_imag = predicted[1:2, :lines] + predicted[0:1, lines:]

    spec_in[n - 1] = spec_out[me]
    arrived = spec_in.at[pl.ds(0, n - 1)]
    pltpu.make_async_copy(arrived, arrived, spec_recv).wait()
    spectra = jnp.sum(spec_in[...], 0) * (1.0 / math.sqrt(ticks * n))
    real = jnp.concatenate([spectra[i : i + 1] for i in range(tiles)], 1)
    imag = jnp.concatenate([spectra[tiles + i : tiles + i + 1] for i in range(tiles)], 1)
    real, imag = real - pred_real, imag - pred_imag
    resid = jnp.concatenate(
        [jnp.concatenate([real, imag], 1), jnp.concatenate([imag, -real], 1)], 0
    ).astype(BF16)
    alm = mul(resid, transfer[...])
    for block in range(blocks):
        out_ref[2 * block : 2 * block + 2, :] = alm[:, block * LANES : (block + 1) * LANES]

    for buffer, sem in ((comp_in, comp_send), (spec_in, spec_send)):
        sent = buffer.at[pl.ds(0, n - 1)]
        pltpu.make_async_copy(sent, sent, sem).wait()


def body(vis, transfer, band_start, comp_index, comp_amp):
    n = lax.axis_size("ma")
    ticks, _, lines = vis.shape
    m_local, _, _, width = transfer.shape
    count = comp_index.shape[0]
    tiles = lines // LANES
    blocks = width // LANES
    assert m_local == 1 and lines % LANES == 0 and width % LANES == 0 and count <= LANES
    pieces = 4
    assert ticks * 2 * tiles % (8 * pieces) == 0
    assert (ticks * n) & (ticks * n - 1) == 0
    flat_vis = (
        vis.reshape(ticks, 2, tiles, LANES).transpose(0, 2, 1, 3).reshape(ticks * 2 * tiles, LANES)
    )
    out = pl.pallas_call(
        functools.partial(kernel, n, ticks, tiles, count, width, pieces),
        out_shape=pltpu.VMEM((2 * blocks, LANES), F32),
        in_specs=[
            pl.BlockSpec(memory_space=pltpu.SMEM),
        ]
        + [pl.BlockSpec(memory_space=pltpu.HBM)] * 4,
        out_specs=pl.BlockSpec(memory_space=pltpu.VMEM),
        scratch_shapes=[
            pltpu.VMEM(flat_vis.shape, F32),
            pltpu.VMEM((2 * lines, width), BF16),
            pltpu.VMEM((1, count), jnp.int32),
            pltpu.VMEM((2, count), jnp.int32),
            pltpu.VMEM((4, LANES), jnp.int32),
            pltpu.VMEM((n, 4, LANES), jnp.int32),
            pltpu.VMEM((n, 2 * tiles, LANES), F32),
            pltpu.VMEM((n, 2 * tiles, LANES), F32),
        ]
        + [pltpu.SemaphoreType.DMA((pieces,))]
        + [pltpu.SemaphoreType.DMA] * 7,
        compiler_params=pltpu.CompilerParams(
            collective_id=0, has_side_effects=True, vmem_limit_bytes=40 * 1024 * 1024
        ),
        cost_estimate=pl.CostEstimate(
            flops=2 * 2 * n * ticks * 2 * lines + 8 * lines * width * 2,
            bytes_accessed=vis.size * 4 + transfer.size * 2,
            transcendentals=0,
        ),
    )(
        band_start,
        *(
            pltpu.with_memory_space_constraint(operand, pltpu.HBM)
            for operand in (
                flat_vis,
                transfer.reshape(2 * lines, width),
                comp_index.reshape(1, count),
                comp_amp.T,
            )
        ),
    )
    return out.reshape(blocks, 2, LANES).transpose(1, 0, 2).reshape(1, 2, width)


def solution(mesh):
    in_specs = (
        P(("grp", "ma"), None, None),
        P(("grp", "ma"), None, None, None),
        P("grp"),
        P(("grp", "ma")),
        P(("grp", "ma"), None),
    )
    out_specs = P(("grp", "ma"), None, None)
    return jax.shard_map(body, mesh=mesh, in_specs=in_specs, out_specs=out_specs, check_vma=False)
```

```python
import functools
import math

import jax
import jax.numpy as jnp
from jax import lax
from jax.experimental import pallas as pl
from jax.experimental.pallas import tpu as pltpu
from jax.sharding import PartitionSpec as P

LANES = 128
F32 = jnp.float32
BF16 = jnp.bfloat16
MESH = pl.DeviceIdType.MESH


def trig_pair(order_start, tick_start, modes, ticks, period):
    order = order_start + lax.broadcasted_iota(jnp.int32, (modes, ticks), 0)
    tick = tick_start + lax.broadcasted_iota(jnp.int32, (modes, ticks), 1)
    phase = (order * tick) & (period - 1)
    quarter = period // 4
    shift = quarter.bit_length() - 1
    quadrant = (phase + quarter // 2) >> shift
    x = (phase - (quadrant << shift)).astype(F32) * (2.0 * math.pi / period)
    z = x * x
    sin_x = x * (1.0 + z * (-1.0 / 6 + z * (1.0 / 120 + z * (-1.0 / 5040 + z * (1.0 / 362880)))))
    cos_x = 1.0 + z * (-0.5 + z * (1.0 / 24 + z * (-1.0 / 720 + z * (1.0 / 40320))))
    swap = (quadrant & 1) == 1
    cos = jnp.where(swap, sin_x, cos_x)
    sin = jnp.where(swap, cos_x, sin_x)
    cos = jnp.where(((quadrant + 1) & 2) == 2, -cos, cos)
    sin = jnp.where((quadrant & 2) == 2, -sin, sin)
    return cos, sin


def split(values):
    high = values.astype(BF16)
    return high, (values - high.astype(F32)).astype(BF16)


def mul(a, b, contract=((1,), (0,))):
    return lax.dot_general(a, b, (contract, ((), ())), preferred_element_type=F32)


def kernel(
    n, ticks, tiles, count, width, pieces,
    start_ref, vis_hbm, transfer_hbm, index_hbm, amp_hbm, out_ref,
    vis, transfer, index_ref, amp_ref, comp_out, comp_in, spec_out, spec_in,
    vis_sem, transfer_sem, index_sem, amp_sem,
    comp_send, comp_recv, spec_send, spec_recv,
):
    me = lax.axis_index("ma")
    index_copy = pltpu.make_async_copy(index_hbm, index_ref, index_sem)
    amp_copy = pltpu.make_async_copy(amp_hbm, amp_ref, amp_sem)
    piece = vis.shape[0] // pieces
    vis_copies = []
    for i in range(pieces):
        part = pl.ds(i * piece, piece)
        vis_copies.append(pltpu.make_async_copy(vis_hbm.at[part], vis.at[part], vis_sem.at[i]))
    transfer_copy = pltpu.make_async_copy(transfer_hbm, transfer, transfer_sem)

    def peers(step):
        if n <= 32:
            for offset in range(1, n):
                step(offset)
        else:
            pl.loop(1, n)(step)

    def peer(offset):
        target = me + offset
        return jnp.where(target >= n, target - n, target)

    barrier = pltpu.get_barrier_semaphore()

    def greet(offset):
        pl.semaphore_signal(barrier, inc=1, device_id={"ma": peer(offset)}, device_id_type=MESH)

    peers(greet)
    for copy in (index_copy, amp_copy, *vis_copies, transfer_copy):
        copy.start()

    cos, sin = trig_pair(start_ref[0], me * ticks, n, ticks, ticks * n)
    (cos_high, cos_low), (sin_high, sin_low) = split(cos), split(sin)
    high_rows = jnp.concatenate([cos_high, sin_high], 0)
    all_rows = jnp.concatenate([cos_high, sin_high, cos_low, sin_low], 0)

    comp_out[...] = jnp.full(comp_out.shape, -1, jnp.int32)
    index_copy.wait()
    amp_copy.wait()
    comp_out[0:1, 0:count] = index_ref[...]
    comp_out[1:3, 0:count] = amp_ref[...]
    comp_in[(n - 1) * 8 : n * 8, :] = comp_out[...]
    def transform(some_tiles):
        for tile in some_tiles:
            parts = [vis[pl.ds(2 * tile + c, ticks, stride=2 * tiles), :] for c in range(2)]
            high, low = split(jnp.concatenate(parts, 1))
            product = mul(all_rows, high)
            product = product[: 2 * n] + product[2 * n :] + mul(high_rows, low)
            real = product[:n, :LANES] + product[n:, LANES:]
            imag = product[:n, LANES:] - product[n:, :LANES]
            spec_out[:, tile, :] = real
            spec_out[:, tiles + tile, :] = imag

    for copy in vis_copies:
        copy.wait()
    transform(range(tiles // 2))
    pl.semaphore_wait(barrier, n - 1)

    def send_comp(offset):
        pltpu.make_async_remote_copy(
            src_ref=comp_out, dst_ref=comp_in.at[pl.ds(pl.multiple_of((offset - 1) * 8, 8), 8)],
            send_sem=comp_send, recv_sem=comp_recv,
            device_id={"ma": peer(offset)}, device_id_type=MESH,
        ).start()

    peers(send_comp)

    transform(range(tiles // 2, tiles))

    def send_spec(offset):
        pltpu.make_async_remote_copy(
            src_ref=spec_out.at[peer(offset)], dst_ref=spec_in.at[offset - 1],
            send_sem=spec_send, recv_sem=spec_recv,
            device_id={"ma": peer(offset)}, device_id_type=MESH,
        ).start()

    peers(send_spec)

    arrived = comp_in.at[pl.ds(0, (n - 1) * 8)]
    pltpu.make_async_copy(arrived, arrived, comp_recv).wait()
    fields = [comp_in[pl.ds(row, n, stride=8), :] for row in range(3)]
    if 2 * count == LANES and n % 2 == 0:
        fields = [jnp.concatenate([f[: n // 2, :count], f[n // 2 :, :count]], 1) for f in fields]
    index = fields[0] - me * width
    blocks = width // LANES
    row_id = lax.broadcasted_iota(jnp.int32, (2 * blocks, LANES), 0)
    low_id = lax.broadcasted_iota(jnp.int32, (LANES, LANES), 0)
    weights, places = [], []
    for chunk in range(index.shape[0]):
        at = index[chunk : chunk + 1]
        amp = jnp.where(
            (row_id & 1) == 1, fields[2][chunk : chunk + 1], fields[1][chunk : chunk + 1]
        )
        amp = jnp.where((at >> 7) == (row_id >> 1), amp, 0)
        halves = jnp.concatenate([amp >> 6, amp & 63], 0)
        weights.append(halves.astype(F32).astype(BF16))
        places.append(jnp.where((at & 127) == low_id, 1.0, 0.0).astype(BF16))
    halves = mul(jnp.concatenate(weights, 1), jnp.concatenate(places, 1), ((1,), (1,)))
    halves = halves.astype(jnp.int32)
    summed = halves[: 2 * blocks] * 64 + halves[2 * blocks :]
    model = summed.astype(F32) * (1.0 / 1024.0)
    model = jnp.concatenate([model[2 * i : 2 * i + 2] for i in range(blocks)], 1).astype(BF16)

    transfer_copy.wait()
    lines = tiles * LANES
    predicted = mul(model, transfer[...], ((1,), (1,)))
    pred_real = predicted[0:1, :lines] - predicted[1:2, lines:]
    pred_imag = predicted[1:2, :lines] + predicted[0:1, lines:]

    spec_in[n - 1] = spec_out[me]
    arrived = spec_in.at[pl.ds(0, n - 1)]
    pltpu.make_async_copy(arrived, arrived, spec_recv).wait()
    spectra = jnp.sum(spec_in[...], 0) * (1.0 / math.sqrt(ticks * n))
    real = jnp.concatenate([spectra[i : i + 1] for i in range(tiles)], 1)
    imag = jnp.concatenate([spectra[tiles + i : tiles + i + 1] for i in range(tiles)], 1)
    real, imag = real - pred_real, imag - pred_imag
    resid = jnp.concatenate(
        [jnp.concatenate([real, imag], 1), jnp.concatenate([imag, -real], 1)], 0
    ).astype(BF16)
    alm = mul(resid, transfer[...])
    for block in range(blocks):
        out_ref[2 * block : 2 * block + 2, :] = alm[:, block * LANES : (block + 1) * LANES]

    for buffer, sem in ((comp_in, comp_send), (spec_in, spec_send)):
        sent = buffer.at[pl.ds(0, buffer.shape[0] // n * (n - 1))]
        pltpu.make_async_copy(sent, sent, sem).wait()


def body(vis, transfer, band_start, comp_index, comp_amp):
    n = lax.axis_size("ma")
    ticks, _, lines = vis.shape
    m_local, _, _, width = transfer.shape
    count = comp_index.shape[0]
    tiles = lines // LANES
    blocks = width // LANES
    assert m_local == 1 and lines % LANES == 0 and width % LANES == 0 and count <= LANES
    pieces = 4
    assert ticks * 2 * tiles % (8 * pieces) == 0
    assert (ticks * n) & (ticks * n - 1) == 0
    flat_vis = (
        vis.reshape(ticks, 2, tiles, LANES).transpose(0, 2, 1, 3).reshape(ticks * 2 * tiles, LANES)
    )
    out = pl.pallas_call(
        functools.partial(kernel, n, ticks, tiles, count, width, pieces),
        out_shape=pltpu.VMEM((2 * blocks, LANES), F32),
        in_specs=[
            pl.BlockSpec(memory_space=pltpu.SMEM),
        ]
        + [pl.BlockSpec(memory_space=pltpu.HBM)] * 4,
        out_specs=pl.BlockSpec(memory_space=pltpu.VMEM),
        scratch_shapes=[
            pltpu.VMEM(flat_vis.shape, F32),
            pltpu.VMEM((2 * lines, width), BF16),
            pltpu.VMEM((1, count), jnp.int32),
            pltpu.VMEM((2, count), jnp.int32),
            pltpu.VMEM((8, LANES), jnp.int32),
            pltpu.VMEM((n * 8, LANES), jnp.int32),
            pltpu.VMEM((n, 2 * tiles, LANES), F32),
            pltpu.VMEM((n, 2 * tiles, LANES), F32),
        ]
        + [pltpu.SemaphoreType.DMA((pieces,))]
        + [pltpu.SemaphoreType.DMA] * 7,
        compiler_params=pltpu.CompilerParams(
            collective_id=0, has_side_effects=True, vmem_limit_bytes=40 * 1024 * 1024
        ),
        cost_estimate=pl.CostEstimate(
            flops=2 * 2 * n * ticks * 2 * lines + 8 * lines * width * 2,
            bytes_accessed=vis.size * 4 + transfer.size * 2,
            transcendentals=0,
        ),
    )(
        band_start,
        *(
            pltpu.with_memory_space_constraint(operand, pltpu.HBM)
            for operand in (
                flat_vis,
                transfer.reshape(2 * lines, width),
                comp_index.reshape(1, count),
                comp_amp.T,
            )
        ),
    )
    return out.reshape(blocks, 2, LANES).transpose(1, 0, 2).reshape(1, 2, width)


def solution(mesh):
    in_specs = (
        P(("grp", "ma"), None, None),
        P(("grp", "ma"), None, None, None),
        P("grp"),
        P(("grp", "ma")),
        P(("grp", "ma"), None),
    )
    out_specs = P(("grp", "ma"), None, None)
    return jax.shard_map(body, mesh=mesh, in_specs=in_specs, out_specs=out_specs, check_vma=False)
```

```python
import functools
import math

import jax
import jax.numpy as jnp
from jax import lax
from jax.experimental import pallas as pl
from jax.experimental.pallas import tpu as pltpu
from jax.sharding import PartitionSpec as P

LANES = 128
F32 = jnp.float32
BF16 = jnp.bfloat16
MESH = pl.DeviceIdType.MESH


def trig_pair(order_start, tick_start, modes, ticks, period):
    order = order_start + lax.broadcasted_iota(jnp.int32, (modes, ticks), 0)
    tick = tick_start + lax.broadcasted_iota(jnp.int32, (modes, ticks), 1)
    phase = (order * tick) & (period - 1)
    quarter = period // 4
    shift = quarter.bit_length() - 1
    quadrant = (phase + quarter // 2) >> shift
    x = (phase - (quadrant << shift)).astype(F32) * (2.0 * math.pi / period)
    z = x * x
    sin_x = x * (1.0 + z * (-1.0 / 6 + z * (1.0 / 120 + z * (-1.0 / 5040 + z * (1.0 / 362880)))))
    cos_x = 1.0 + z * (-0.5 + z * (1.0 / 24 + z * (-1.0 / 720 + z * (1.0 / 40320))))
    swap = (quadrant & 1) == 1
    cos = jnp.where(swap, sin_x, cos_x)
    sin = jnp.where(swap, cos_x, sin_x)
    cos = jnp.where(((quadrant + 1) & 2) == 2, -cos, cos)
    sin = jnp.where((quadrant & 2) == 2, -sin, sin)
    return cos, sin


def split(values):
    high = values.astype(BF16)
    return high, (values - high.astype(F32)).astype(BF16)


def mul(a, b, contract=((1,), (0,))):
    return lax.dot_general(a, b, (contract, ((), ())), preferred_element_type=F32)


def kernel(
    n, ticks, tiles, count, width, pieces,
    start_ref, vis_hbm, transfer_hbm, index_hbm, amp_hbm, out_ref,
    vis, transfer, index_ref, amp_ref, comp_out, comp_in, spec_out, spec_in,
    vis_sem, transfer_sem, index_sem, amp_sem,
    comp_send, comp_recv, spec_send, spec_recv,
):
    me = lax.axis_index("ma")
    index_copy = pltpu.make_async_copy(index_hbm, index_ref, index_sem)
    amp_copy = pltpu.make_async_copy(amp_hbm, amp_ref, amp_sem)
    piece = vis.shape[0] // pieces
    vis_copies = []
    for i in range(pieces):
        part = pl.ds(i * piece, piece)
        vis_copies.append(pltpu.make_async_copy(vis_hbm.at[part], vis.at[part], vis_sem.at[i]))
    transfer_copy = pltpu.make_async_copy(transfer_hbm, transfer, transfer_sem)

    def peers(step):
        if n <= 32:
            for offset in range(1, n):
                step(offset)
        else:
            pl.loop(1, n)(step)

    def peer(offset):
        target = me + offset
        return jnp.where(target >= n, target - n, target)

    barrier = pltpu.get_barrier_semaphore()

    def greet(offset):
        pl.semaphore_signal(barrier, inc=1, device_id={"ma": peer(offset)}, device_id_type=MESH)

    peers(greet)
    for copy in (index_copy, amp_copy, *vis_copies, transfer_copy):
        copy.start()

    cos, sin = trig_pair(start_ref[0], me * ticks, n, ticks, ticks * n)
    (cos_high, cos_low), (sin_high, sin_low) = split(cos), split(sin)
    high_rows = jnp.concatenate([cos_high, sin_high], 0)
    all_rows = jnp.concatenate([cos_high, sin_high, cos_low, sin_low], 0)

    comp_out[...] = jnp.full(comp_out.shape, -1, jnp.int32)
    index_copy.wait()
    amp_copy.wait()
    comp_out[0:1, 0:count] = index_ref[...]
    comp_out[1:3, 0:count] = amp_ref[...]
    comp_in[n - 1] = comp_out[...]
    pl.semaphore_wait(barrier, n - 1)

    def send_comp(offset):
        pltpu.make_async_remote_copy(
            src_ref=comp_out, dst_ref=comp_in.at[offset - 1],
            send_sem=comp_send, recv_sem=comp_recv,
            device_id={"ma": peer(offset)}, device_id_type=MESH,
        ).start()

    peers(send_comp)

    for copy in vis_copies:
        copy.wait()
    rows = 2 * tiles
    for tile in range(tiles):
        parts = [vis[pl.ds(2 * tile + c, ticks, stride=rows), :] for c in range(2)]
        high, low = split(jnp.concatenate(parts, 1))
        product = mul(all_rows, high)
        product = product[: 2 * n] + product[2 * n :] + mul(high_rows, low)
        real = product[:n, :LANES] + product[n:, LANES:]
        imag = product[:n, LANES:] - product[n:, :LANES]
        spec_out[:, tile, :] = real
        spec_out[:, tiles + tile, :] = imag

    def send_spec(offset):
        pltpu.make_async_remote_copy(
            src_ref=spec_out.at[peer(offset)], dst_ref=spec_in.at[offset - 1],
            send_sem=spec_send, recv_sem=spec_recv,
            device_id={"ma": peer(offset)}, device_id_type=MESH,
        ).start()

    peers(send_spec)

    arrived = comp_in.at[pl.ds(0, n - 1)]
    pltpu.make_async_copy(arrived, arrived, comp_recv).wait()
    fields = [comp_in[:, row, :] for row in range(3)]
    if 2 * count == LANES and n % 2 == 0:
        fields = [jnp.concatenate([f[: n // 2, :count], f[n // 2 :, :count]], 1) for f in fields]
    index = fields[0] - me * width
    blocks = width // LANES
    row_id = lax.broadcasted_iota(jnp.int32, (2 * blocks, LANES), 0)
    low_id = lax.broadcasted_iota(jnp.int32, (LANES, LANES), 0)
    weights, places = [], []
    for chunk in range(index.shape[0]):
        at = index[chunk : chunk + 1]
        amp = jnp.where(
            (row_id & 1) == 1, fields[2][chunk : chunk + 1], fields[1][chunk : chunk + 1]
        )
        amp = jnp.where((at >> 7) == (row_id >> 1), amp, 0)
        halves = jnp.concatenate([amp >> 6, amp & 63], 0)
        weights.append(halves.astype(F32).astype(BF16))
        places.append(jnp.where((at & 127) == low_id, 1.0, 0.0).astype(BF16))
    halves = mul(jnp.concatenate(weights, 1), jnp.concatenate(places, 1), ((1,), (1,)))
    halves = halves.astype(jnp.int32)
    summed = halves[: 2 * blocks] * 64 + halves[2 * blocks :]
    model = summed.astype(F32) * (1.0 / 1024.0)
    model = jnp.concatenate([model[2 * i : 2 * i + 2] for i in range(blocks)], 1).astype(BF16)

    transfer_copy.wait()
    lines = tiles * LANES
    predicted = mul(model, transfer[...], ((1,), (1,)))
    pred_real = predicted[0:1, :lines] - predicted[1:2, lines:]
    pred_imag = predicted[1:2, :lines] + predicted[0:1, lines:]

    spec_in[n - 1] = spec_out[me]
    arrived = spec_in.at[pl.ds(0, n - 1)]
    pltpu.make_async_copy(arrived, arrived, spec_recv).wait()
    spectra = jnp.sum(spec_in[...], 0) * (1.0 / math.sqrt(ticks * n))
    real = jnp.concatenate([spectra[i : i + 1] for i in range(tiles)], 1)
    imag = jnp.concatenate([spectra[tiles + i : tiles + i + 1] for i in range(tiles)], 1)
    real, imag = real - pred_real, imag - pred_imag
    resid = jnp.concatenate(
        [jnp.concatenate([real, imag], 1), jnp.concatenate([imag, -real], 1)], 0
    ).astype(BF16)
    alm = mul(resid, transfer[...])
    for block in range(blocks):
        out_ref[2 * block : 2 * block + 2, :] = alm[:, block * LANES : (block + 1) * LANES]

    for buffer, sem in ((comp_in, comp_send), (spec_in, spec_send)):
        sent = buffer.at[pl.ds(0, n - 1)]
        pltpu.make_async_copy(sent, sent, sem).wait()


def body(vis, transfer, band_start, comp_index, comp_amp):
    n = lax.axis_size("ma")
    ticks, _, lines = vis.shape
    m_local, _, _, width = transfer.shape
    count = comp_index.shape[0]
    tiles = lines // LANES
    blocks = width // LANES
    assert m_local == 1 and lines % LANES == 0 and width % LANES == 0 and count <= LANES
    pieces = 4
    assert ticks * 2 * tiles % (8 * pieces) == 0
    assert (ticks * n) & (ticks * n - 1) == 0
    flat_vis = (
        vis.reshape(ticks, 2, tiles, LANES).transpose(0, 2, 1, 3).reshape(ticks * 2 * tiles, LANES)
    )
    out = pl.pallas_call(
        functools.partial(kernel, n, ticks, tiles, count, width, pieces),
        out_shape=pltpu.VMEM((2 * blocks, LANES), F32),
        in_specs=[
            pl.BlockSpec(memory_space=pltpu.SMEM),
        ]
        + [pl.BlockSpec(memory_space=pltpu.HBM)] * 4,
        out_specs=pl.BlockSpec(memory_space=pltpu.VMEM),
        scratch_shapes=[
            pltpu.VMEM(flat_vis.shape, F32),
            pltpu.VMEM((2 * lines, width), BF16),
            pltpu.VMEM((1, count), jnp.int32),
            pltpu.VMEM((2, count), jnp.int32),
            pltpu.VMEM((4, LANES), jnp.int32),
            pltpu.VMEM((n, 4, LANES), jnp.int32),
            pltpu.VMEM((n, 2 * tiles, LANES), F32),
            pltpu.VMEM((n, 2 * tiles, LANES), F32),
        ]
        + [pltpu.SemaphoreType.DMA((pieces,))]
        + [pltpu.SemaphoreType.DMA] * 7,
        compiler_params=pltpu.CompilerParams(
            collective_id=0, has_side_effects=True, vmem_limit_bytes=40 * 1024 * 1024
        ),
        cost_estimate=pl.CostEstimate(
            flops=2 * 2 * n * ticks * 2 * lines + 8 * lines * width * 2,
            bytes_accessed=vis.size * 4 + transfer.size * 2,
            transcendentals=0,
        ),
    )(
        band_start,
        *(
            pltpu.with_memory_space_constraint(operand, pltpu.HBM)
            for operand in (
                flat_vis,
                transfer.reshape(2 * lines, width),
                comp_index.reshape(1, count),
                comp_amp.T,
            )
        ),
    )
    return out.reshape(blocks, 2, LANES).transpose(1, 0, 2).reshape(1, 2, width)


def solution(mesh):
    in_specs = (
        P(("grp", "ma"), None, None),
        P(("grp", "ma"), None, None, None),
        P("grp"),
        P(("grp", "ma")),
        P(("grp", "ma"), None),
    )
    out_specs = P(("grp", "ma"), None, None)
    return jax.shard_map(body, mesh=mesh, in_specs=in_specs, out_specs=out_specs, check_vma=False)
```
